32 devices in a mesh: groups: 2 (over x), member: 8 (over z, y), tile: 2 (over core).
Axes of the slice: x: 2, y: 2, z: 4, core: 2. Of those that a mesh axis runs over, the one named last changes fastest.
Arguments:
- perturbations: bfloat16 [32, 3, 50, 16384], P(('groups', 'member'), None, None, 'tile'), parts along dimension 0, may hold values from -6 to 6
- control: float32 [32, 50, 16384], P(('groups', 'member'), None, 'tile'), parts along dimension 0, may hold values from -6 to 6
- loc_sqrt: float32 [50, 50], replicated, may hold values from 0 to 1
- gate_points: int32 [8, 32768], P(None, ('groups', 'member', 'tile')), parts along dimension 1, may hold values from 0 to 409599, as said below
- gate_weights: float32 [8, 32768], P(None, ('groups', 'member', 'tile')), parts along dimension 1, may hold values from 0.05 to 1
- gate_azimuth: float32 [32768], P(('groups', 'member', 'tile')), parts along dimension 0, may hold values from -3.140625 to 3.140625
- gate_elevation: float32 [32768], P(('groups', 'member', 'tile')), parts along dimension 0, may hold values from 0 to 0.5
- innovation: float32 [32768], P(('groups', 'member', 'tile')), parts along dimension 0, may hold values from -10 to 10
- obs_weight: float32 [32768], P(('groups', 'member', 'tile')), parts along dimension 0, may hold values from 0.25 to 4
- gate_counts: int32 [32], P(('groups', 'member', 'tile')), parts along dimension 0, may hold values from 256 to 1024, as said below
Outputs:
- gradient: float32 [32, 50, 16384], P(('groups', 'member'), None, 'tile'), parts along dimension 0
- gate_residual: float32 [32768], P(('groups', 'member', 'tile')), parts along dimension 0
The draws below stay inside these ranges and needn't reach their ends.
There are 2 independent parts, one for each index of `groups`. The reference program is written for one: setup_inputs(seed, part) draws one part's arguments, and reference() takes and returns one part's arrays. A program takes and returns all parts, laid end to end along the dimension named above; an argument that names none is the same for every part. Nothing has to cross between parts.
Inputs may be any that keep to these rules, and one draw needn't show every extreme that they name: `gate_points`: column g lists the eight corners of one grid box of gate g's tile: with base level z, base x and base y, corner (a, b, c), c fastest, is (z + a) * 8192 + (x + b) * 128 + y + c. `gate_counts`: one block is full in every draw.
All inputs are finite; a program needn't handle non-finite values.
Results may differ from the reference program's by a relative error of at most 0.0003.
Values sent between devices are 32-bit elements; how exact they have to be, the bound alone decides.
A program may use at most 128 MiB of HBM per device.

```python
import math
import jax
import jax.numpy as jnp
from jax import lax

NZ = 50
TILE_X = 64
TILE_Y = 128
GATE_DEV = 1024
CELL_DEV = 8192
CELLS = 16384
MEMBERS = 16
GATE_BLOCKS = 16
GATES = 16384
N_TILE = 2


def draw_loc_sqrt(key, part):
    key = jax.random.fold_in(key, 11)
    level_row = lax.broadcasted_iota(jnp.int32, (NZ, NZ), 0)
    level_col = lax.broadcasted_iota(jnp.int32, (NZ, NZ), 1)
    distance = jnp.abs(level_row - level_col).astype(jnp.float32)
    factor = jax.random.uniform(key, (NZ, NZ), jnp.float32, 0.2, 1.0)
    return 0.25 * jnp.where(level_row == level_col, 3.0 + factor, jnp.exp(-distance / 2.0) * factor)


def draw_gate_points(key, part):
    key = jax.random.fold_in(key, 23)
    level_key, east_key, north_key = jax.random.split(key, 3)
    base_level = jax.random.randint(level_key, (GATES,), 0, NZ - 1)
    base_east = jax.random.randint(east_key, (GATES,), 0, TILE_X - 1)
    base_north = jax.random.randint(north_key, (GATES,), 0, TILE_Y - 1)
    base_level = base_level.at[0].set(NZ - 2).at[1].set(0)
    base_east = base_east.at[0].set(TILE_X - 2).at[1].set(0)
    base_north = base_north.at[0].set(TILE_Y - 2).at[1].set(0)
    corner = jnp.arange(8, dtype=jnp.int32)
    up_step = (corner // 4)[:, None]
    east_step = (corner // 2 % 2)[:, None]
    north_step = (corner % 2)[:, None]
    flat_index = (base_level[None, :] + up_step) * CELL_DEV + (base_east[None, :] + east_step) * TILE_Y + base_north[None, :] + north_step
    return flat_index.astype(jnp.int32)


def draw_gate_counts(key, part):
    key = jax.random.fold_in(key, 37)
    count_key, full_key = jax.random.split(key, 2)
    counts = jax.random.randint(count_key, (GATE_BLOCKS,), GATE_DEV // 4, GATE_DEV + 1)
    fullest = jax.random.randint(full_key, (), 0, GATE_BLOCKS)
    lowest = (fullest + 1) % GATE_BLOCKS
    block_number = jnp.arange(GATE_BLOCKS, dtype=jnp.int32)
    counts = jnp.where(block_number == fullest, GATE_DEV, counts)
    counts = jnp.where(block_number == lowest, GATE_DEV // 4, counts)
    return counts.astype(jnp.int32)


def block_scale(stream_key, extent, shards, smallest, top_value):
    factor_of, own = 1.0, jax.random.fold_in(stream_key, 6)
    for dim, parts in shards:
        draws = jnp.exp(jax.random.uniform(jax.random.fold_in(own, dim), (parts,), jnp.float32, smallest / len(shards), top_value / len(shards)))
        factor_of = factor_of * jnp.repeat(draws, extent[dim] // parts).reshape([-1 if axis == dim else 1 for axis in range(len(extent))])
    return factor_of


def gaussian(rng, extent, scale, bound, cuts=(), kind=jnp.bfloat16):
    result = jax.random.normal(rng, extent, jnp.float32) * scale
    if len(cuts) > 0:
        result = block_scale(rng, extent, cuts, -0.22, 0.18) * result
    return jnp.clip(result, min=-bound, max=bound).astype(kind)


def setup_inputs(seed: int = 0, part: int = 0) -> dict:
    keys = jax.random.split(jax.random.key(seed), 11)
    own_keys = jax.random.split(jax.random.fold_in(keys[10], part), 11)
    return {
        "perturbations": gaussian(own_keys[0], (MEMBERS, 3, NZ, CELLS), 1.0, 6.0, ((0, 8), (3, 2))),
        "control": gaussian(own_keys[1], (MEMBERS, NZ, CELLS), 1.0, 6.0, ((0, 8), (2, 2)), jnp.float32),
        "loc_sqrt": draw_loc_sqrt(jax.random.fold_in(keys[10], 71), part),
        "gate_points": draw_gate_points(jax.random.fold_in(jax.random.fold_in(keys[10], part), 71), part),
        "gate_weights": jnp.clip(0.05 + 0.95 * jax.random.uniform(own_keys[4], (8, GATES), jnp.float32) ** block_scale(own_keys[4], (8, GATES), ((1, 16),), -0.2, 0.2), 0.05, 1.0),
        "gate_azimuth": jnp.clip(jax.random.uniform(own_keys[5], (GATES,), jnp.float32, -3.140625, 3.140625), -3.140625, 3.140625),
        "gate_elevation": jnp.clip(0.5 * jax.random.uniform(own_keys[6], (GATES,), jnp.float32) ** block_scale(own_keys[6], (GATES,), ((0, 16),), -0.2, 0.2), 0.0, 0.5),
        "innovation": gaussian(own_keys[7], (GATES,), 2.0, 10.0, ((0, 16),), jnp.float32),
        "obs_weight": jnp.clip(jnp.exp(math.log(4.0) - 2.7725887 * jax.random.uniform(own_keys[8], (GATES,), jnp.float32) ** block_scale(own_keys[8], (GATES,), ((0, 16),), -0.2, 0.2)), 0.25, 4.0),
        "gate_counts": draw_gate_counts(jax.random.fold_in(jax.random.fold_in(keys[10], part), 71), part),
    }


def radial_terms(azimuth, elevation):
    horizontal = jnp.cos(elevation)
    return jnp.stack([horizontal * jnp.sin(azimuth), horizontal * jnp.cos(azimuth), jnp.sin(elevation)])

def observe(field_flat, corner_index, corner_weight, coefficients):
    picked = field_flat[:, corner_index]
    return lax.optimization_barrier(jnp.sum(corner_weight * lax.optimization_barrier(jnp.sum(coefficients[:, None, :] * picked, axis=0)), axis=0))

def spread(corner_index, corner_weight, coefficients, weighted, total_size):
    amount = corner_weight * weighted[None, :]
    contributions = coefficients[:, None, :] * amount[None, :, :]
    empty = jnp.zeros((3, total_size), jnp.float32)
    return empty.at[:, corner_index.reshape(-1)].add(contributions.reshape(3, -1))

def reference(perturbations, control, loc_sqrt, gate_points, gate_weights, gate_azimuth, gate_elevation, innovation, obs_weight, gate_counts):
    spread_factor = (MEMBERS - 1) ** (-0.5)
    localized = jnp.einsum('zy,kyj->kzj', loc_sqrt, control, precision=lax.Precision.HIGHEST)
    increment = spread_factor * lax.optimization_barrier(jnp.sum(perturbations.astype(jnp.float32) * localized[:, None], axis=0))
    tile_size = NZ * CELL_DEV
    fields = increment.reshape(3, NZ, N_TILE, CELL_DEV).transpose(0, 2, 1, 3).reshape(3, N_TILE * tile_size)
    gate_number = jnp.arange(GATES, dtype=jnp.int32)
    gate_block = gate_number // GATE_DEV
    tile_of_gate = gate_block % N_TILE
    slot_index = gate_number % GATE_DEV
    live_mask = (slot_index < gate_counts[gate_block]).astype(jnp.float32)
    global_index = (tile_of_gate[None, :] * tile_size + gate_points).astype(jnp.int32)
    coefficients = radial_terms(gate_azimuth, gate_elevation)
    modelled = observe(fields, global_index, gate_weights, coefficients)
    gate_residual = live_mask * (modelled - innovation)
    adjoint_flat = spread(global_index, gate_weights, coefficients, obs_weight * gate_residual, N_TILE * tile_size)
    adjoint = adjoint_flat.reshape(3, N_TILE, NZ, CELL_DEV).transpose(0, 2, 1, 3).reshape(3, NZ, CELLS)
    weighted_mix = lax.optimization_barrier(jnp.sum(perturbations.astype(jnp.float32) * adjoint[None], axis=1))
    gradient = control + spread_factor * jnp.einsum('zy,kzj->kyj', loc_sqrt, weighted_mix, precision=lax.Precision.HIGHEST)
    return (gradient, gate_residual)
```

```python
import functools

import jax
import jax.numpy as jnp
from jax import lax
from jax.experimental import pallas as pl
from jax.experimental.pallas import tpu as pltpu
from jax.sharding import PartitionSpec as P

LANES = 128
LEVEL_PAD = 56
DEPTH = 64
X_STEP = LEVEL_PAD * 3
CHUNK = 16
BUFFERS = 4
X_BLOCK = 8
VMEM = 56 * 1024 * 1024


def split(value):
    high = value.astype(jnp.bfloat16)
    low = (value - high.astype(jnp.float32)).astype(jnp.bfloat16)
    return high, low


def level_product(matrix, value):
    m_high, m_low = split(matrix)
    v_high, v_low = split(value)
    left = jnp.concatenate([m_high, m_high, m_low], axis=1)
    right = jnp.concatenate([v_high, v_low, v_high], axis=0)
    return jnp.dot(left, right, preferred_element_type=jnp.float32)


def field_kernel(loc_ref, control_ref, pert_ref, field_ref, padded):
    members, levels, width = control_ref.shape

    @pl.when(pl.program_id(0) == 0)
    def _():
        padded[...] = jnp.zeros_like(padded)

    total = [None] * 3
    for k in range(members):
        padded[0:levels, :] = control_ref[k]
        localized = level_product(loc_ref[...], padded[...])[0:levels]
        for c in range(3):
            term = pert_ref[k, c].astype(jnp.float32) * localized
            total[c] = term if k == 0 else total[c] + term
    for x in range(width // LANES):
        start = x * X_STEP
        field_ref[start + 144 : start + X_STEP, :] = jnp.zeros((X_STEP - 144, LANES), jnp.float32)
        for c in range(3):
            field_ref[pl.ds(start + c, levels, stride=3), :] = total[c][
                :, x * LANES : (x + 1) * LANES
            ]


def gate_factors(meta_ref, block, lanes):
    weight = meta_ref[block, 0:8, lanes]
    coeff = meta_ref[block, 8:16, lanes]
    row = lax.broadcasted_iota(jnp.int32, (8, LANES), 0)
    component = row % 3
    by_row = jnp.where(
        component == 0, coeff[0:1], jnp.where(component == 1, coeff[1:2], coeff[2:3])
    )
    factors = {}
    for b in range(2):
        for c in range(2):
            p = 2 * b + c
            corner = jnp.where(
                row < 3, weight[p : p + 1], jnp.where(row < 6, weight[4 + p : 5 + p], 0.0)
            )
            factors[b, c] = corner * by_row
    return factors


def over_groups(counts_ref, slots, visit):
    def block_body(block, carry):
        count = counts_ref[block]

        def group_body(group, inner):
            left = jnp.minimum(count - group * LANES, LANES)
            visit(block, group, (left + CHUNK - 1) // CHUNK)
            return inner

        lax.fori_loop(0, (count + LANES - 1) // LANES, group_body, 0)
        return carry

    lax.fori_loop(0, counts_ref.shape[0], block_body, 0)


def gather_kernel(counts_ref, index_ref, meta_ref, field_ref, out_ref):
    slots = meta_ref.shape[2]
    groups = slots // LANES
    out_ref[...] = jnp.zeros_like(out_ref)
    lane = lax.broadcasted_iota(jnp.int32, (8, LANES), 1)

    def visit(block, group, chunks):
        first = block * slots + group * LANES

        def chunk_body(chunk, acc):
            a00, a01, a10, a11 = acc
            slot = chunk * CHUNK
            shifted = lane - slot
            here = shifted == 0
            for i in range(CHUNK):
                packed = index_ref[first + slot + i]
                row = packed >> 7
                shift = packed & 127
                near = pltpu.roll(field_ref[pl.ds(row, 8), :], shift, axis=1)
                far = pltpu.roll(field_ref[pl.ds(row + X_STEP, 8), :], shift, axis=1)
                if i < CHUNK - 1:
                    after = shifted == i + 1
                else:
                    after = lane == ((slot + CHUNK) & 127)
                a00 = jnp.where(here, near, a00)
                a01 = jnp.where(after, near, a01)
                a10 = jnp.where(here, far, a10)
                a11 = jnp.where(after, far, a11)
                here = after
            return a00, a01, a10, a11

        zero = jnp.zeros((8, LANES), jnp.float32)
        a00, a01, a10, a11 = lax.fori_loop(0, chunks, chunk_body, (zero, zero, zero, zero))
        factors = gate_factors(meta_ref, block, pl.ds(pl.multiple_of(group * LANES, LANES), LANES))
        value = (
            a00 * factors[0, 0]
            + pltpu.roll(a01, LANES - 1, axis=1) * factors[0, 1]
            + a10 * factors[1, 0]
            + pltpu.roll(a11, LANES - 1, axis=1) * factors[1, 1]
        )
        out_ref[pl.ds(block * groups + group, 1), :] = jnp.sum(value, axis=0, keepdims=True)

    over_groups(counts_ref, slots, visit)


def scatter_kernel(
    factor, counts_ref, index_ref, meta_ref, weighted_ref, loc_ref, control_ref, pert_ref,
    out_ref, buffers, padded,
):
    members, levels, width = control_ref.shape
    slots = meta_ref.shape[2]
    groups = slots // LANES
    step = pl.program_id(0)

    @pl.when(step == 0)
    def _():
        padded[...] = jnp.zeros_like(padded)
        rows = buffers.shape[1]
        per = X_STEP

        def clear(i, carry):
            at = pl.ds(pl.multiple_of(i * per, per), per)
            for j in range(BUFFERS):
                buffers[j, at, :] = jnp.zeros((per, LANES), jnp.float32)
            return carry

        lax.fori_loop(0, rows // per, clear, 0)
        lane = lax.broadcasted_iota(jnp.int32, (8, LANES), 1)

        def visit(block, group, chunks):
            first = block * slots + group * LANES
            factors = gate_factors(
                meta_ref, block, pl.ds(pl.multiple_of(group * LANES, LANES), LANES)
            )
            amount = weighted_ref[pl.ds(block * groups + group, 1), :]
            a00 = factors[0, 0] * amount
            a01 = pltpu.roll(factors[0, 1] * amount, 1, axis=1)
            a10 = factors[1, 0] * amount
            a11 = pltpu.roll(factors[1, 1] * amount, 1, axis=1)

            def chunk_body(chunk, carry):
                slot = chunk * CHUNK
                shifted = lane - slot
                here = shifted == 0
                for i0 in range(0, CHUNK, BUFFERS):
                    added = []
                    for j in range(BUFFERS):
                        i = i0 + j
                        packed = index_ref[first + slot + i]
                        row = packed >> 7
                        shift = (-packed) & 127
                        if i < CHUNK - 1:
                            after = shifted == i + 1
                        else:
                            after = lane == ((slot + CHUNK) & 127)
                        near = jnp.where(here, a00, jnp.where(after, a01, 0.0))
                        far = jnp.where(here, a10, jnp.where(after, a11, 0.0))
                        here = after
                        added.append(
                            (
                                pl.ds(row, 8),
                                pl.ds(row + X_STEP, 8),
                                pltpu.roll(near, shift, axis=1),
                                pltpu.roll(far, shift, axis=1),
                            )
                        )
                    held = [
                        (buffers[j, added[j][0], :], buffers[j, added[j][1], :])
                        for j in range(BUFFERS)
                    ]
                    for j in range(BUFFERS):
                        buffers[j, added[j][0], :] = held[j][0] + added[j][2]
                        buffers[j, added[j][1], :] = held[j][1] + added[j][3]
                return carry

            lax.fori_loop(0, chunks, chunk_body, 0)

        over_groups(counts_ref, slots, visit)

    adjoint = []
    for c in range(3):
        pieces = []
        for x in range(width // LANES):
            at = pl.ds(step * (width // LANES) * X_STEP + x * X_STEP + c, LEVEL_PAD, stride=3)
            piece = buffers[0, at, :]
            for j in range(1, BUFFERS):
                piece = piece + buffers[j, at, :]
            pieces.append(piece[0:levels])
        adjoint.append(jnp.concatenate(pieces, axis=1))
    for k in range(members):
        mix = pert_ref[k, 0].astype(jnp.float32) * adjoint[0]
        for c in range(1, 3):
            mix = mix + pert_ref[k, c].astype(jnp.float32) * adjoint[c]
        padded[0:levels, :] = mix
        product = level_product(loc_ref[...], padded[...])
        out_ref[k] = control_ref[k] + factor * product[0:levels]


def whole(shape):
    return pl.BlockSpec(shape, lambda *i: (0,) * len(shape))


def local(
    perturbations,
    control,
    loc_sqrt,
    gate_points,
    gate_weights,
    gate_azimuth,
    gate_elevation,
    innovation,
    obs_weight,
    gate_counts,
):
    mem_dev, components, levels, tile_cells = perturbations.shape
    slots = gate_points.shape[1]
    axis = lax.axis_size("member")
    factor = (mem_dev * axis - 1) ** (-0.5)
    columns = tile_cells // LANES
    rows = columns * X_STEP
    width = X_BLOCK * LANES

    horizontal = jnp.cos(gate_elevation)
    own = jnp.concatenate(
        [
            gate_weights,
            jnp.stack(
                [
                    horizontal * jnp.sin(gate_azimuth),
                    horizontal * jnp.cos(gate_azimuth),
                    jnp.sin(gate_elevation),
                    innovation,
                    obs_weight,
                    gate_points[0].astype(jnp.float32),
                    jnp.broadcast_to(gate_counts.astype(jnp.float32), (slots,)),
                    jnp.zeros((slots,), jnp.float32),
                ]
            ),
        ],
        axis=0,
    )
    meta = lax.all_gather(own, "member")
    base = meta[:, 13].astype(jnp.int32)
    level = base // tile_cells
    column = base % tile_cells // LANES
    position = base % LANES
    slot = jnp.arange(slots, dtype=jnp.int32)
    row = (column * LEVEL_PAD + level) * 3
    index = (row * LANES + (slot[None] - position) % LANES).reshape(-1)
    counts = meta[:, 14, 0].astype(jnp.int32)

    loc_pad = jnp.pad(loc_sqrt, ((0, DEPTH - levels), (0, DEPTH - levels)))
    pert_spec = pl.BlockSpec((mem_dev, 3, levels, width), lambda i: (0, 0, 0, i))
    control_spec = pl.BlockSpec((mem_dev, levels, width), lambda i: (0, 0, i))
    smem = pl.BlockSpec(memory_space=pltpu.SMEM)
    vmem = pl.BlockSpec(memory_space=pltpu.VMEM)
    field = pl.pallas_call(
        field_kernel,
        grid=(tile_cells // width,),
        out_shape=jax.ShapeDtypeStruct((rows, LANES), jnp.float32),
        in_specs=[whole((DEPTH, DEPTH)), control_spec, pert_spec],
        out_specs=pl.BlockSpec((X_BLOCK * X_STEP, LANES), lambda i: (i, 0)),
        scratch_shapes=[pltpu.VMEM((DEPTH, width), jnp.float32)],
        compiler_params=pltpu.CompilerParams(vmem_limit_bytes=VMEM),
        cost_estimate=pl.CostEstimate(
            flops=6 * tile_cells * DEPTH * DEPTH * mem_dev, bytes_accessed=14 << 20, transcendentals=0
        ),
        name="field",
    )(loc_pad, control, perturbations)

    groups = axis * slots // LANES
    partial = pl.pallas_call(
        gather_kernel,
        out_shape=jax.ShapeDtypeStruct((groups, LANES), jnp.float32),
        in_specs=[smem, smem, vmem, vmem],
        out_specs=vmem,
        compiler_params=pltpu.CompilerParams(vmem_limit_bytes=VMEM),
        name="gather",
    )(counts, index, meta, field)

    modelled = factor * lax.psum(partial, "member").reshape(axis, slots)
    live = (slot[None] < counts[:, None]).astype(jnp.float32)
    residual = live * (modelled - meta[:, 11])
    weighted = (meta[:, 12] * residual).reshape(groups, LANES)
    gate_residual = lax.dynamic_index_in_dim(residual, lax.axis_index("member"), 0, keepdims=False)

    gradient = pl.pallas_call(
        functools.partial(scatter_kernel, factor),
        grid=(tile_cells // width,),
        out_shape=jax.ShapeDtypeStruct((mem_dev, levels, tile_cells), jnp.float32),
        in_specs=[
            smem,
            smem,
            whole(meta.shape),
            whole((groups, LANES)),
            whole((DEPTH, DEPTH)),
            control_spec,
            pert_spec,
        ],
        out_specs=control_spec,
        scratch_shapes=[
            pltpu.VMEM((BUFFERS, rows, LANES), jnp.float32),
            pltpu.VMEM((DEPTH, width), jnp.float32),
        ],
        compiler_params=pltpu.CompilerParams(vmem_limit_bytes=VMEM),
        name="scatter",
    )(counts, index, meta, weighted, loc_pad.T, control, perturbations)
    return (gradient, gate_residual)


def solution(mesh):
    by_gate = P(("groups", "member", "tile"))
    return jax.shard_map(
        local,
        mesh=mesh,
        in_specs=(
            P(("groups", "member"), None, None, "tile"),
            P(("groups", "member"), None, "tile"),
            P(),
            P(None, ("groups", "member", "tile")),
            P(None, ("groups", "member", "tile")),
            by_gate,
            by_gate,
            by_gate,
            by_gate,
            by_gate,
        ),
        out_specs=(P(("groups", "member"), None, "tile"), by_gate),
        check_vma=False,
    )
```

```python
import functools

import jax
import jax.numpy as jnp
from jax import lax
from jax.experimental import pallas as pl
from jax.experimental.pallas import tpu as pltpu
from jax.sharding import PartitionSpec as P

LANES = 128
LEVEL_PAD = 56
DEPTH = 64
X_STEP = LEVEL_PAD * 3
CHUNK = 64
BUFFERS = 4
X_BLOCK = 8
MESH = pl.DeviceIdType.MESH
VMEM = 56 * 1024 * 1024


def split(value):
    high = value.astype(jnp.bfloat16)
    low = (value - high.astype(jnp.float32)).astype(jnp.bfloat16)
    return high, low


def level_product(matrix, value):
    m_high, m_low = split(matrix)
    v_high, v_low = split(value)
    left = jnp.concatenate([m_high, m_high, m_low], axis=1)
    right = jnp.concatenate([v_high, v_low, v_high], axis=0)
    return jnp.dot(left, right, preferred_element_type=jnp.float32)


def exchange(own_ref, slots_ref, send_sem, recv_sem):
    axis, me = lax.axis_size("member"), lax.axis_index("member")
    barrier = pltpu.get_barrier_semaphore()
    for d in range(1, axis):
        pl.semaphore_signal(
            barrier, inc=1, device_id={"member": lax.rem(me + d, axis)}, device_id_type=MESH
        )
    pl.semaphore_wait(barrier, axis - 1)
    copies = []
    for d in range(1, axis):
        copy = pltpu.make_async_remote_copy(
            src_ref=own_ref,
            dst_ref=slots_ref.at[me],
            send_sem=send_sem.at[d - 1],
            recv_sem=recv_sem.at[d - 1],
            device_id={"member": lax.rem(me + d, axis)},
            device_id_type=MESH,
        )
        copy.start()
        copies.append(copy)
    slots_ref[me] = own_ref[...]
    for copy in copies:
        copy.wait()


def gates_kernel(
    tile_cells, own_ref, meta_ref, index_ref, counts_ref, side_ref, slots_ref, send_sem, recv_sem
):
    axis, fields, slots = slots_ref.shape
    per = slots // LANES
    exchange(own_ref, slots_ref, send_sem, recv_sem)
    slot = lax.broadcasted_iota(jnp.int32, (1, slots), 1)
    for d in range(axis):
        meta_ref[d] = slots_ref[d]
        base = slots_ref[d, 13:14, :].astype(jnp.int32)
        count = slots_ref[d, 14:15, :].astype(jnp.int32)
        level = lax.div(base, jnp.int32(tile_cells))
        inside = base - level * tile_cells
        column = lax.div(inside, jnp.int32(LANES))
        position = inside - column * LANES
        index = (column * LEVEL_PAD + level) * (3 * LANES) + ((slot - position) & (LANES - 1))
        live = jnp.where(slot < count, 1.0, 0.0)
        innovation = slots_ref[d, 11:12, :]
        weight = slots_ref[d, 12:13, :]
        counts_ref[d : d + 1, :] = count[:, 0:LANES]
        for q in range(per):
            row = d * per + q
            lanes = slice(q * LANES, (q + 1) * LANES)
            index_ref[row : row + 1, :] = index[:, lanes]
            side_ref[0, row : row + 1, :] = live[:, lanes]
            side_ref[1, row : row + 1, :] = innovation[:, lanes]
            side_ref[2, row : row + 1, :] = weight[:, lanes]


def residual_kernel(
    factor, partial_ref, side_ref, weighted_ref, residual_ref, slots_ref, whole_ref, send_sem, recv_sem
):
    axis = slots_ref.shape[0]
    per = residual_ref.shape[0]
    exchange(partial_ref, slots_ref, send_sem, recv_sem)
    total = slots_ref[0]
    for d in range(1, axis):
        total = total + slots_ref[d]
    residual = side_ref[0] * (factor * total - side_ref[1])
    weighted_ref[...] = side_ref[2] * residual
    whole_ref[...] = residual.reshape(whole_ref.shape)
    residual_ref[...] = whole_ref[lax.axis_index("member")]


def field_kernel(loc_ref, control_ref, pert_ref, field_ref, padded):
    members, levels, width = control_ref.shape

    @pl.when(pl.program_id(0) == 0)
    def _():
        padded[...] = jnp.zeros_like(padded)

    total = [None] * 3
    for k in range(members):
        padded[0:levels, :] = control_ref[k]
        localized = level_product(loc_ref[...], padded[...])[0:levels]
        for c in range(3):
            term = pert_ref[k, c].astype(jnp.float32) * localized
            total[c] = term if k == 0 else total[c] + term
    for x in range(width // LANES):
        start = x * X_STEP
        field_ref[start + 144 : start + X_STEP, :] = jnp.zeros((X_STEP - 144, LANES), jnp.float32)
        for c in range(3):
            field_ref[pl.ds(start + c, levels, stride=3), :] = total[c][
                :, x * LANES : (x + 1) * LANES
            ]


def gate_factors(meta_ref, block, lanes):
    weight = meta_ref[block, 0:8, lanes]
    coeff = meta_ref[block, 8:16, lanes]
    row = lax.broadcasted_iota(jnp.int32, (8, LANES), 0)
    component = row % 3
    by_row = jnp.where(
        component == 0, coeff[0:1], jnp.where(component == 1, coeff[1:2], coeff[2:3])
    )
    factors = {}
    for b in range(2):
        for c in range(2):
            p = 2 * b + c
            corner = jnp.where(
                row < 3, weight[p : p + 1], jnp.where(row < 6, weight[4 + p : 5 + p], 0.0)
            )
            factors[b, c] = corner * by_row
    return factors


def over_groups(counts_ref, slots, visit):
    def block_body(block, carry):
        count = counts_ref[block * LANES]

        def group_body(group, inner):
            left = jnp.minimum(count - group * LANES, LANES)
            visit(block, group, (left + CHUNK - 1) // CHUNK)
            return inner

        lax.fori_loop(0, (count + LANES - 1) // LANES, group_body, 0)
        return carry

    lax.fori_loop(0, counts_ref.shape[0] // LANES, block_body, 0)


def gather_kernel(counts_ref, index_ref, meta_ref, field_ref, out_ref):
    slots = meta_ref.shape[2]
    groups = slots // LANES
    out_ref[...] = jnp.zeros_like(out_ref)
    lane = lax.broadcasted_iota(jnp.int32, (8, LANES), 1)

    def visit(block, group, chunks):
        first = block * slots + group * LANES

        def chunk_body(chunk, acc):
            a00, a01, a10, a11 = acc
            slot = chunk * CHUNK
            shifted = lane - slot
            here = shifted == 0
            for i in range(CHUNK):
                packed = index_ref[first + slot + i]
                row = packed >> 7
                shift = packed & 127
                near = pltpu.roll(field_ref[pl.ds(row, 8), :], shift, axis=1)
                far = pltpu.roll(field_ref[pl.ds(row + X_STEP, 8), :], shift, axis=1)
                if i < CHUNK - 1:
                    after = shifted == i + 1
                else:
                    after = lane == ((slot + CHUNK) & 127)
                a00 = jnp.where(here, near, a00)
                a01 = jnp.where(after, near, a01)
                a10 = jnp.where(here, far, a10)
                a11 = jnp.where(after, far, a11)
                here = after
            return a00, a01, a10, a11

        zero = jnp.zeros((8, LANES), jnp.float32)
        a00, a01, a10, a11 = lax.fori_loop(0, chunks, chunk_body, (zero, zero, zero, zero))
        factors = gate_factors(meta_ref, block, pl.ds(pl.multiple_of(group * LANES, LANES), LANES))
        value = (
            a00 * factors[0, 0]
            + pltpu.roll(a01, LANES - 1, axis=1) * factors[0, 1]
            + a10 * factors[1, 0]
            + pltpu.roll(a11, LANES - 1, axis=1) * factors[1, 1]
        )
        out_ref[pl.ds(block * groups + group, 1), :] = jnp.sum(value, axis=0, keepdims=True)

    over_groups(counts_ref, slots, visit)


def scatter_kernel(
    factor, counts_ref, index_ref, meta_ref, weighted_ref, loc_ref, control_ref, pert_ref,
    out_ref, buffers, padded,
):
    members, levels, width = control_ref.shape
    slots = meta_ref.shape[2]
    groups = slots // LANES
    step = pl.program_id(0)

    @pl.when(step == 0)
    def _():
        padded[...] = jnp.zeros_like(padded)
        rows = buffers.shape[1]
        per = X_STEP

        def clear(i, carry):
            at = pl.ds(pl.multiple_of(i * per, per), per)
            for j in range(BUFFERS):
                buffers[j, at, :] = jnp.zeros((per, LANES), jnp.float32)
            return carry

        lax.fori_loop(0, rows // per, clear, 0)
        lane = lax.broadcasted_iota(jnp.int32, (8, LANES), 1)

        def visit(block, group, chunks):
            first = block * slots + group * LANES
            factors = gate_factors(
                meta_ref, block, pl.ds(pl.multiple_of(group * LANES, LANES), LANES)
            )
            amount = weighted_ref[pl.ds(block * groups + group, 1), :]
            a00 = factors[0, 0] * amount
            a01 = pltpu.roll(factors[0, 1] * amount, 1, axis=1)
            a10 = factors[1, 0] * amount
            a11 = pltpu.roll(factors[1, 1] * amount, 1, axis=1)

            def chunk_body(chunk, carry):
                slot = chunk * CHUNK
                shifted = lane - slot
                here = shifted == 0
                for i0 in range(0, CHUNK, BUFFERS):
                    added = []
                    for j in range(BUFFERS):
                        i = i0 + j
                        packed = index_ref[first + slot + i]
                        row = packed >> 7
                        shift = (-packed) & 127
                        if i < CHUNK - 1:
                            after = shifted == i + 1
                        else:
                            after = lane == ((slot + CHUNK) & 127)
                        near = jnp.where(here, a00, jnp.where(after, a01, 0.0))
                        far = jnp.where(here, a10, jnp.where(after, a11, 0.0))
                        here = after
                        added.append(
                            (
                                pl.ds(row, 8),
                                pl.ds(row + X_STEP, 8),
                                pltpu.roll(near, shift, axis=1),
                                pltpu.roll(far, shift, axis=1),
                            )
                        )
                    held = [
                        (buffers[j, added[j][0], :], buffers[j, added[j][1], :])
                        for j in range(BUFFERS)
                    ]
                    for j in range(BUFFERS):
                        buffers[j, added[j][0], :] = held[j][0] + added[j][2]
                        buffers[j, added[j][1], :] = held[j][1] + added[j][3]
                return carry

            lax.fori_loop(0, chunks, chunk_body, 0)

        over_groups(counts_ref, slots, visit)

    adjoint = []
    for c in range(3):
        pieces = []
        for x in range(width // LANES):
            at = pl.ds(step * (width // LANES) * X_STEP + x * X_STEP + c, LEVEL_PAD, stride=3)
            piece = buffers[0, at, :]
            for j in range(1, BUFFERS):
                piece = piece + buffers[j, at, :]
            pieces.append(piece[0:levels])
        adjoint.append(jnp.concatenate(pieces, axis=1))
    for k in range(members):
        mix = pert_ref[k, 0].astype(jnp.float32) * adjoint[0]
        for c in range(1, 3):
            mix = mix + pert_ref[k, c].astype(jnp.float32) * adjoint[c]
        padded[0:levels, :] = mix
        product = level_product(loc_ref[...], padded[...])
        out_ref[k] = control_ref[k] + factor * product[0:levels]


def whole(shape):
    return pl.BlockSpec(shape, lambda *i: (0,) * len(shape))


def local(
    perturbations,
    control,
    loc_sqrt,
    gate_points,
    gate_weights,
    gate_azimuth,
    gate_elevation,
    innovation,
    obs_weight,
    gate_counts,
):
    mem_dev, components, levels, tile_cells = perturbations.shape
    slots = gate_points.shape[1]
    axis = lax.axis_size("member")
    factor = (mem_dev * axis - 1) ** (-0.5)
    columns = tile_cells // LANES
    rows = columns * X_STEP
    width = X_BLOCK * LANES

    horizontal = jnp.cos(gate_elevation)
    own = jnp.concatenate(
        [
            gate_weights,
            jnp.stack(
                [
                    horizontal * jnp.sin(gate_azimuth),
                    horizontal * jnp.cos(gate_azimuth),
                    jnp.sin(gate_elevation),
                    innovation,
                    obs_weight,
                    gate_points[0].astype(jnp.float32),
                    jnp.broadcast_to(gate_counts.astype(jnp.float32), (slots,)),
                    jnp.zeros((slots,), jnp.float32),
                ]
            ),
        ],
        axis=0,
    )
    groups = axis * slots // LANES
    vmem = pl.BlockSpec(memory_space=pltpu.VMEM)
    smem = pl.BlockSpec(memory_space=pltpu.SMEM)
    semaphores = [pltpu.SemaphoreType.DMA((axis - 1,)), pltpu.SemaphoreType.DMA((axis - 1,))]
    meta, index, counts, side = pl.pallas_call(
        functools.partial(gates_kernel, tile_cells),
        out_shape=(
            jax.ShapeDtypeStruct((axis, 16, slots), jnp.float32),
            jax.ShapeDtypeStruct((groups, LANES), jnp.int32),
            jax.ShapeDtypeStruct((axis, LANES), jnp.int32),
            jax.ShapeDtypeStruct((3, groups, LANES), jnp.float32),
        ),
        in_specs=[vmem],
        out_specs=(vmem, vmem, vmem, vmem),
        scratch_shapes=[pltpu.VMEM((axis, 16, slots), jnp.float32), *semaphores],
        compiler_params=pltpu.CompilerParams(
            collective_id=0, has_side_effects=True, vmem_limit_bytes=VMEM
        ),
        name="gates",
    )(own)
    index, counts = index.reshape(-1), counts.reshape(-1)

    loc_pad = jnp.pad(loc_sqrt, ((0, DEPTH - levels), (0, DEPTH - levels)))
    pert_spec = pl.BlockSpec((mem_dev, 3, levels, width), lambda i: (0, 0, 0, i))
    control_spec = pl.BlockSpec((mem_dev, levels, width), lambda i: (0, 0, i))
    field = pl.pallas_call(
        field_kernel,
        grid=(tile_cells // width,),
        out_shape=jax.ShapeDtypeStruct((rows, LANES), jnp.float32),
        in_specs=[whole((DEPTH, DEPTH)), control_spec, pert_spec],
        out_specs=pl.BlockSpec((X_BLOCK * X_STEP, LANES), lambda i: (i, 0)),
        scratch_shapes=[pltpu.VMEM((DEPTH, width), jnp.float32)],
        compiler_params=pltpu.CompilerParams(vmem_limit_bytes=VMEM),
        cost_estimate=pl.CostEstimate(
            flops=6 * tile_cells * DEPTH * DEPTH * mem_dev, bytes_accessed=14 << 20, transcendentals=0
        ),
        name="field",
    )(loc_pad, control, perturbations)

    partial = pl.pallas_call(
        gather_kernel,
        out_shape=jax.ShapeDtypeStruct((groups, LANES), jnp.float32),
        in_specs=[smem, smem, vmem, vmem],
        out_specs=vmem,
        compiler_params=pltpu.CompilerParams(vmem_limit_bytes=VMEM),
        name="gather",
    )(counts, index, meta, field)

    weighted, residual = pl.pallas_call(
        functools.partial(residual_kernel, factor),
        out_shape=(
            jax.ShapeDtypeStruct((groups, LANES), jnp.float32),
            jax.ShapeDtypeStruct((slots // LANES, LANES), jnp.float32),
        ),
        in_specs=[vmem, vmem],
        out_specs=(vmem, vmem),
        scratch_shapes=[
            pltpu.VMEM((axis, groups, LANES), jnp.float32),
            pltpu.VMEM((axis, slots // LANES, LANES), jnp.float32),
            *semaphores,
        ],
        compiler_params=pltpu.CompilerParams(
            collective_id=1, has_side_effects=True, vmem_limit_bytes=VMEM
        ),
        name="residual",
    )(partial, side)
    gate_residual = residual.reshape(slots)

    gradient = pl.pallas_call(
        functools.partial(scatter_kernel, factor),
        grid=(tile_cells // width,),
        out_shape=jax.ShapeDtypeStruct((mem_dev, levels, tile_cells), jnp.float32),
        in_specs=[
            smem,
            smem,
            whole(meta.shape),
            whole((groups, LANES)),
            whole((DEPTH, DEPTH)),
            control_spec,
            pert_spec,
        ],
        out_specs=control_spec,
        scratch_shapes=[
            pltpu.VMEM((BUFFERS, rows, LANES), jnp.float32),
            pltpu.VMEM((DEPTH, width), jnp.float32),
        ],
        compiler_params=pltpu.CompilerParams(vmem_limit_bytes=VMEM),
        name="scatter",
    )(counts, index, meta, weighted, loc_pad.T, control, perturbations)
    return (gradient, gate_residual)


def solution(mesh):
    by_gate = P(("groups", "member", "tile"))
    return jax.shard_map(
        local,
        mesh=mesh,
        in_specs=(
            P(("groups", "member"), None, None, "tile"),
            P(("groups", "member"), None, "tile"),
            P(),
            P(None, ("groups", "member", "tile")),
            P(None, ("groups", "member", "tile")),
            by_gate,
            by_gate,
            by_gate,
            by_gate,
            by_gate,
        ),
        out_specs=(P(("groups", "member"), None, "tile"), by_gate),
        check_vma=False,
    )
```

```python
import functools

import jax
import jax.numpy as jnp
from jax import lax
from jax.experimental import pallas as pl
from jax.experimental.pallas import tpu as pltpu
from jax.sharding import PartitionSpec as P

LANES = 128
LEVEL_PAD = 56
DEPTH = 64
X_STEP = LEVEL_PAD * 3
CHUNK = 64
BUFFERS = 4
X_BLOCK = 8
MESH = pl.DeviceIdType.MESH
VMEM = 56 * 1024 * 1024


def split(value):
    high = value.astype(jnp.bfloat16)
    low = (value - high.astype(jnp.float32)).astype(jnp.bfloat16)
    return high, low


def level_product(matrix, value):
    m_high, m_low = split(matrix)
    v_high, v_low = split(value)
    left = jnp.concatenate([m_high, m_high, m_low], axis=1)
    right = jnp.concatenate([v_high, v_low, v_high], axis=0)
    return jnp.dot(left, right, preferred_element_type=jnp.float32)


def greet():
    axis, me = lax.axis_size("member"), lax.axis_index("member")
    barrier = pltpu.get_barrier_semaphore()
    for d in range(1, axis):
        pl.semaphore_signal(
            barrier, inc=1, device_id={"member": lax.rem(me + d, axis)}, device_id_type=MESH
        )
    pl.semaphore_wait(barrier, axis - 1)


def copies_out(source, slots_ref, send_sem, recv_sem):
    axis, me = lax.axis_size("member"), lax.axis_index("member")
    copies = []
    for d in range(1, axis):
        to = lax.rem(me + d, axis)
        copies.append(
            pltpu.make_async_remote_copy(
                src_ref=source(to),
                dst_ref=slots_ref.at[me],
                send_sem=send_sem.at[d - 1],
                recv_sem=recv_sem.at[d - 1],
                device_id={"member": to},
                device_id_type=MESH,
            )
        )
    return copies


def field_kernel(
    tile_cells, loc_ref, control_ref, pert_ref, points_ref, weights_ref, azimuth_ref,
    elevation_ref, innovation_ref, obs_ref, count_ref,
    field_ref, meta_ref, index_ref, counts_ref, side_ref,
    padded, pert_rows, own_ref, slots_ref, send_sem, recv_sem,
):
    axis, fields, slots = slots_ref.shape
    per = slots // LANES
    me = lax.axis_index("member")
    step = pl.program_id(0)

    @pl.when(step == 0)
    def _():
        padded[...] = jnp.zeros_like(padded)
        own_ref[0:8, :] = weights_ref[...]
        horizontal = jnp.cos(elevation_ref[...])
        own_ref[8:9, :] = horizontal * jnp.sin(azimuth_ref[...])
        own_ref[9:10, :] = horizontal * jnp.cos(azimuth_ref[...])
        own_ref[10:11, :] = jnp.sin(elevation_ref[...])
        own_ref[11:12, :] = innovation_ref[...]
        own_ref[12:13, :] = obs_ref[...]
        own_ref[13:14, :] = points_ref[0:1, :].astype(jnp.float32)
        own_ref[14:15, :] = jnp.full((1, slots), count_ref[0], jnp.int32).astype(jnp.float32)
        own_ref[15:16, :] = jnp.zeros((1, slots), jnp.float32)
        greet()
        for copy in copies_out(lambda to: own_ref, slots_ref, send_sem, recv_sem):
            copy.start()
        slots_ref[me] = own_ref[...]

    levels, across, lanes = control_ref.shape
    control_rows = control_ref.reshape(levels * across, lanes)
    for r in range(across):
        padded[0:levels, r * LANES : (r + 1) * LANES] = control_rows[
            pl.ds(r, levels, stride=across), :
        ]
    localized = level_product(loc_ref[...], padded[...])[0:levels]
    members = across // X_BLOCK
    for c in range(3):
        pert_rows[...] = pert_ref[c].astype(jnp.float32).reshape(levels * across, lanes)
        for x in range(X_BLOCK):
            total = None
            for k in range(members):
                r = x * members + k
                term = (
                    pert_rows[pl.ds(r, levels, stride=across), :]
                    * localized[:, r * LANES : (r + 1) * LANES]
                )
                total = term if k == 0 else total + term
            if c == 0:
                field_ref[x * X_STEP + 144 : (x + 1) * X_STEP, :] = jnp.zeros(
                    (X_STEP - 144, LANES), jnp.float32
                )
            field_ref[pl.ds(x * X_STEP + c, levels, stride=3), :] = total

    @pl.when(step == pl.num_programs(0) - 1)
    def _():
        for copy in copies_out(lambda to: own_ref, slots_ref, send_sem, recv_sem):
            copy.wait()
        slot = lax.broadcasted_iota(jnp.int32, (1, slots), 1)
        for d in range(axis):
            meta_ref[d] = slots_ref[d]
            base = slots_ref[d, 13:14, :].astype(jnp.int32)
            count = slots_ref[d, 14:15, :].astype(jnp.int32)
            level = lax.div(base, jnp.int32(tile_cells))
            inside = base - level * tile_cells
            column = lax.div(inside, jnp.int32(LANES))
            position = inside - column * LANES
            index = (column * LEVEL_PAD + level) * (3 * LANES) + ((slot - position) & (LANES - 1))
            live = jnp.where(slot < count, 1.0, 0.0)
            innovation = slots_ref[d, 11:12, :]
            weight = slots_ref[d, 12:13, :]
            counts_ref[d : d + 1, :] = count[:, 0:LANES]
            for q in range(per):
                row = d * per + q
                at = slice(q * LANES, (q + 1) * LANES)
                index_ref[row : row + 1, :] = index[:, at]
                side_ref[0, row : row + 1, :] = live[:, at]
                side_ref[1, row : row + 1, :] = innovation[:, at]
                side_ref[2, row : row + 1, :] = weight[:, at]


def residual_kernel(
    factor, partial_ref, side_ref, weighted_ref, residual_ref,
    parts_ref, done_ref, send_sem, recv_sem, send_done, recv_done,
):
    axis, per, lanes = parts_ref.shape
    me = lax.axis_index("member")
    greet()
    sums = copies_out(
        lambda to: partial_ref.at[pl.ds(pl.multiple_of(to * per, per), per), :],
        parts_ref, send_sem, recv_sem,
    )
    for copy in sums:
        copy.start()
    own = pl.ds(pl.multiple_of(me * per, per), per)
    parts_ref[me] = partial_ref[own, :]
    for copy in sums:
        copy.wait()
    total = parts_ref[0]
    for d in range(1, axis):
        total = total + parts_ref[d]
    residual = side_ref[0, own, :] * (factor * total - side_ref[1, own, :])
    residual_ref[...] = residual
    done_ref[me] = side_ref[2, own, :] * residual
    results = copies_out(lambda to: done_ref.at[me], done_ref, send_done, recv_done)
    for copy in results:
        copy.start()
    for copy in results:
        copy.wait()
    for d in range(axis):
        weighted_ref[d * per : (d + 1) * per, :] = done_ref[d]


def gate_factors(meta_ref, block, lanes):
    weight = meta_ref[block, 0:8, lanes]
    coeff = meta_ref[block, 8:16, lanes]
    row = lax.broadcasted_iota(jnp.int32, (8, LANES), 0)
    component = row % 3
    by_row = jnp.where(
        component == 0, coeff[0:1], jnp.where(component == 1, coeff[1:2], coeff[2:3])
    )
    factors = {}
    for b in range(2):
        for c in range(2):
            p = 2 * b + c
            corner = jnp.where(
                row < 3, weight[p : p + 1], jnp.where(row < 6, weight[4 + p : 5 + p], 0.0)
            )
            factors[b, c] = corner * by_row
    return factors


def over_groups(counts_ref, slots, visit):
    def block_body(block, carry):
        count = counts_ref[block * LANES]

        def group_body(group, inner):
            left = jnp.minimum(count - group * LANES, LANES)
            visit(block, group, (left + CHUNK - 1) // CHUNK)
            return inner

        lax.fori_loop(0, (count + LANES - 1) // LANES, group_body, 0)
        return carry

    lax.fori_loop(0, counts_ref.shape[0] // LANES, block_body, 0)


def gather_kernel(counts_ref, index_ref, meta_ref, field_ref, out_ref):
    slots = meta_ref.shape[2]
    groups = slots // LANES
    out_ref[...] = jnp.zeros_like(out_ref)
    lane = lax.broadcasted_iota(jnp.int32, (8, LANES), 1)

    def visit(block, group, chunks):
        first = block * slots + group * LANES

        def chunk_body(chunk, acc):
            a00, a01, a10, a11 = acc
            slot = chunk * CHUNK
            shifted = lane - slot
            here = shifted == 0
            for i in range(CHUNK):
                packed = index_ref[first + slot + i]
                row = packed >> 7
                shift = packed & 127
                near = pltpu.roll(field_ref[pl.ds(row, 8), :], shift, axis=1)
                far = pltpu.roll(field_ref[pl.ds(row + X_STEP, 8), :], shift, axis=1)
                if i < CHUNK - 1:
                    after = shifted == i + 1
                else:
                    after = lane == ((slot + CHUNK) & 127)
                a00 = jnp.where(here, near, a00)
                a01 = jnp.where(after, near, a01)
                a10 = jnp.where(here, far, a10)
                a11 = jnp.where(after, far, a11)
                here = after
            return a00, a01, a10, a11

        zero = jnp.zeros((8, LANES), jnp.float32)
        a00, a01, a10, a11 = lax.fori_loop(0, chunks, chunk_body, (zero, zero, zero, zero))
        factors = gate_factors(meta_ref, block, pl.ds(pl.multiple_of(group * LANES, LANES), LANES))
        value = (
            a00 * factors[0, 0]
            + pltpu.roll(a01, LANES - 1, axis=1) * factors[0, 1]
            + a10 * factors[1, 0]
            + pltpu.roll(a11, LANES - 1, axis=1) * factors[1, 1]
        )
        out_ref[pl.ds(block * groups + group, 1), :] = jnp.sum(value, axis=0, keepdims=True)

    over_groups(counts_ref, slots, visit)


def scatter_kernel(
    factor, counts_ref, index_ref, meta_ref, weighted_ref, loc_ref, control_ref, pert_ref,
    out_ref, buffers, padded, pert_rows,
):
    levels, across, lanes = control_ref.shape
    slots = meta_ref.shape[2]
    groups = slots // LANES
    step = pl.program_id(0)

    @pl.when(step == 0)
    def _():
        padded[...] = jnp.zeros_like(padded)
        rows = buffers.shape[1]
        per = X_STEP

        def clear(i, carry):
            at = pl.ds(pl.multiple_of(i * per, per), per)
            for j in range(BUFFERS):
                buffers[j, at, :] = jnp.zeros((per, LANES), jnp.float32)
            return carry

        lax.fori_loop(0, rows // per, clear, 0)
        lane = lax.broadcasted_iota(jnp.int32, (8, LANES), 1)

        def visit(block, group, chunks):
            first = block * slots + group * LANES
            factors = gate_factors(
                meta_ref, block, pl.ds(pl.multiple_of(group * LANES, LANES), LANES)
            )
            amount = weighted_ref[pl.ds(block * groups + group, 1), :]
            a00 = factors[0, 0] * amount
            a01 = pltpu.roll(factors[0, 1] * amount, 1, axis=1)
            a10 = factors[1, 0] * amount
            a11 = pltpu.roll(factors[1, 1] * amount, 1, axis=1)

            def chunk_body(chunk, carry):
                slot = chunk * CHUNK
                shifted = lane - slot
                here = shifted == 0
                for i0 in range(0, CHUNK, BUFFERS):
                    added = []
                    for j in range(BUFFERS):
                        i = i0 + j
                        packed = index_ref[first + slot + i]
                        row = packed >> 7
                        shift = (-packed) & 127
                        if i < CHUNK - 1:
                            after = shifted == i + 1
                        else:
                            after = lane == ((slot + CHUNK) & 127)
                        near = jnp.where(here, a00, jnp.where(after, a01, 0.0))
                        far = jnp.where(here, a10, jnp.where(after, a11, 0.0))
                        here = after
                        added.append(
                            (
                                pl.ds(row, 8),
                                pl.ds(row + X_STEP, 8),
                                pltpu.roll(near, shift, axis=1),
                                pltpu.roll(far, shift, axis=1),
                            )
                        )
                    held = [
                        (buffers[j, added[j][0], :], buffers[j, added[j][1], :])
                        for j in range(BUFFERS)
                    ]
                    for j in range(BUFFERS):
                        buffers[j, added[j][0], :] = held[j][0] + added[j][2]
                        buffers[j, added[j][1], :] = held[j][1] + added[j][3]
                return carry

            lax.fori_loop(0, chunks, chunk_body, 0)

        over_groups(counts_ref, slots, visit)

    members = across // X_BLOCK
    for c in range(3):
        pert_rows[...] = pert_ref[c].astype(jnp.float32).reshape(levels * across, lanes)
        for x in range(X_BLOCK):
            at = pl.ds((step * X_BLOCK + x) * X_STEP + c, levels, stride=3)
            adjoint = buffers[0, at, :]
            for j in range(1, BUFFERS):
                adjoint = adjoint + buffers[j, at, :]
            for k in range(members):
                r = x * members + k
                here = slice(r * LANES, (r + 1) * LANES)
                term = pert_rows[pl.ds(r, levels, stride=across), :] * adjoint
                if c == 0:
                    padded[0:levels, here] = term
                else:
                    padded[0:levels, here] = padded[0:levels, here] + term
    product = level_product(loc_ref[...], padded[...])
    control_rows = control_ref.reshape(levels * across, lanes)
    out_rows = out_ref.reshape(levels * across, lanes)
    for r in range(across):
        at = pl.ds(r, levels, stride=across)
        out_rows[at, :] = (
            control_rows[at, :] + factor * product[0:levels, r * LANES : (r + 1) * LANES]
        )


def whole(shape):
    return pl.BlockSpec(shape, lambda *i: (0,) * len(shape))


def local(
    perturbations,
    control,
    loc_sqrt,
    gate_points,
    gate_weights,
    gate_azimuth,
    gate_elevation,
    innovation,
    obs_weight,
    gate_counts,
):
    mem_dev, components, levels, tile_cells = perturbations.shape
    slots = gate_points.shape[1]
    axis = lax.axis_size("member")
    factor = (mem_dev * axis - 1) ** (-0.5)
    columns = tile_cells // LANES
    rows = columns * X_STEP
    groups = axis * slots // LANES
    vmem = pl.BlockSpec(memory_space=pltpu.VMEM)
    smem = pl.BlockSpec(memory_space=pltpu.SMEM)
    semaphores = [pltpu.SemaphoreType.DMA((axis - 1,)), pltpu.SemaphoreType.DMA((axis - 1,))]
    across = X_BLOCK * mem_dev
    control_view = (
        control.reshape(mem_dev, levels, columns, LANES)
        .transpose(1, 2, 0, 3)
        .reshape(levels, columns * mem_dev, LANES)
    )
    pert_view = (
        perturbations.reshape(mem_dev, 3, levels, columns, LANES)
        .transpose(1, 2, 3, 0, 4)
        .reshape(3, levels, columns * mem_dev, LANES)
    )
    loc_pad = jnp.pad(loc_sqrt, ((0, DEPTH - levels), (0, DEPTH - levels)))
    pert_spec = pl.BlockSpec((3, levels, across, LANES), lambda i: (0, 0, i, 0))
    control_spec = pl.BlockSpec((levels, across, LANES), lambda i: (0, i, 0))
    dense = [
        pltpu.VMEM((DEPTH, across * LANES), jnp.float32),
        pltpu.VMEM((levels * across, LANES), jnp.float32),
    ]
    row = whole((1, slots))
    field, meta, index, counts, side = pl.pallas_call(
        functools.partial(field_kernel, tile_cells),
        grid=(columns // X_BLOCK,),
        out_shape=(
            jax.ShapeDtypeStruct((rows, LANES), jnp.float32),
            jax.ShapeDtypeStruct((axis, 16, slots), jnp.float32),
            jax.ShapeDtypeStruct((groups, LANES), jnp.int32),
            jax.ShapeDtypeStruct((axis, LANES), jnp.int32),
            jax.ShapeDtypeStruct((3, groups, LANES), jnp.float32),
        ),
        in_specs=[
            whole((DEPTH, DEPTH)),
            control_spec,
            pert_spec,
            whole((8, slots)),
            whole((8, slots)),
            row,
            row,
            row,
            row,
            smem,
        ],
        out_specs=(
            pl.BlockSpec((X_BLOCK * X_STEP, LANES), lambda i: (i, 0)),
            whole((axis, 16, slots)),
            whole((groups, LANES)),
            whole((axis, LANES)),
            whole((3, groups, LANES)),
        ),
        scratch_shapes=[
            *dense,
            pltpu.VMEM((16, slots), jnp.float32),
            pltpu.VMEM((axis, 16, slots), jnp.float32),
            *semaphores,
        ],
        compiler_params=pltpu.CompilerParams(
            collective_id=0, has_side_effects=True, vmem_limit_bytes=VMEM
        ),
        name="field",
    )(
        loc_pad,
        control_view,
        pert_view,
        gate_points,
        gate_weights,
        gate_azimuth.reshape(1, slots),
        gate_elevation.reshape(1, slots),
        innovation.reshape(1, slots),
        obs_weight.reshape(1, slots),
        gate_counts,
    )
    index, counts = index.reshape(-1), counts.reshape(-1)

    partial = pl.pallas_call(
        gather_kernel,
        out_shape=jax.ShapeDtypeStruct((groups, LANES), jnp.float32),
        in_specs=[smem, smem, vmem, vmem],
        out_specs=vmem,
        compiler_params=pltpu.CompilerParams(vmem_limit_bytes=VMEM),
        name="gather",
    )(counts, index, meta, field)

    weighted, residual = pl.pallas_call(
        functools.partial(residual_kernel, factor),
        out_shape=(
            jax.ShapeDtypeStruct((groups, LANES), jnp.float32),
            jax.ShapeDtypeStruct((slots // LANES, LANES), jnp.float32),
        ),
        in_specs=[vmem, vmem],
        out_specs=(vmem, vmem),
        scratch_shapes=[
            pltpu.VMEM((axis, slots // LANES, LANES), jnp.float32),
            pltpu.VMEM((axis, slots // LANES, LANES), jnp.float32),
            *semaphores,
            *semaphores,
        ],
        compiler_params=pltpu.CompilerParams(
            collective_id=1, has_side_effects=True, vmem_limit_bytes=VMEM
        ),
        name="residual",
    )(partial, side)
    gate_residual = residual.reshape(slots)

    gradient = pl.pallas_call(
        functools.partial(scatter_kernel, factor),
        grid=(columns // X_BLOCK,),
        out_shape=jax.ShapeDtypeStruct((levels, columns * mem_dev, LANES), jnp.float32),
        in_specs=[
            smem,
            smem,
            whole(meta.shape),
            whole((groups, LANES)),
            whole((DEPTH, DEPTH)),
            control_spec,
            pert_spec,
        ],
        out_specs=control_spec,
        scratch_shapes=[
            pltpu.VMEM((BUFFERS, rows, LANES), jnp.float32),
            *dense,
        ],
        compiler_params=pltpu.CompilerParams(vmem_limit_bytes=VMEM),
        name="scatter",
    )(counts, index, meta, weighted, loc_pad.T, control_view, pert_view)
    gradient = (
        gradient.reshape(levels, columns, mem_dev, LANES)
        .transpose(2, 0, 1, 3)
        .reshape(mem_dev, levels, tile_cells)
    )
    return (gradient, gate_residual)


def solution(mesh):
    by_gate = P(("groups", "member", "tile"))
    return jax.shard_map(
        local,
        mesh=mesh,
        in_specs=(
            P(("groups", "member"), None, None, "tile"),
            P(("groups", "member"), None, "tile"),
            P(),
            P(None, ("groups", "member", "tile")),
            P(None, ("groups", "member", "tile")),
            by_gate,
            by_gate,
            by_gate,
            by_gate,
            by_gate,
        ),
        out_specs=(P(("groups", "member"), None, "tile"), by_gate),
        check_vma=False,
    )
```

```python
import functools

import jax
import jax.numpy as jnp
from jax import lax
from jax.experimental import pallas as pl
from jax.experimental.pallas import tpu as pltpu
from jax.sharding import PartitionSpec as P

LANES = 128
LEVEL_PAD = 56
DEPTH = 64
X_STEP = LEVEL_PAD * 3
CHUNK = 128
BUFFERS = 4
X_BLOCK = 8
FORWARD_STEP = 4
MESH = pl.DeviceIdType.MESH
VMEM = 56 * 1024 * 1024


def split(value):
    high = value.astype(jnp.bfloat16)
    low = (value - high.astype(jnp.float32)).astype(jnp.bfloat16)
    return high, low


def level_product(matrix, value, flipped):
    m_high, m_low = split(matrix)
    v_high, v_low = split(value)
    side = 0 if flipped else 1
    left = jnp.concatenate([m_high, m_high, m_low], axis=side)
    right = jnp.concatenate([v_high, v_low, v_high], axis=0)
    return lax.dot_general(
        left, right, (((side,), (0,)), ((), ())), preferred_element_type=jnp.float32
    )


def pad_matrix(loc_ref, loc_pad):
    levels = loc_ref.shape[0]
    loc_pad[...] = jnp.zeros_like(loc_pad)
    loc_pad[0:levels, 0:levels] = loc_ref[...]


def greet():
    axis, me = lax.axis_size("member"), lax.axis_index("member")
    barrier = pltpu.get_barrier_semaphore()
    for d in range(1, axis):
        pl.semaphore_signal(
            barrier, inc=1, device_id={"member": lax.rem(me + d, axis)}, device_id_type=MESH
        )
    pl.semaphore_wait(barrier, axis - 1)


def copies_out(source, slots_ref, send_sem, recv_sem):
    axis, me = lax.axis_size("member"), lax.axis_index("member")
    copies = []
    for d in range(1, axis):
        to = lax.rem(me + d, axis)
        copies.append(
            pltpu.make_async_remote_copy(
                src_ref=source(to),
                dst_ref=slots_ref.at[me],
                send_sem=send_sem.at[d - 1],
                recv_sem=recv_sem.at[d - 1],
                device_id={"member": to},
                device_id_type=MESH,
            )
        )
    return copies


def block_copies(own_ref, slots_ref, send_sem, recv_sem):
    axis, me = lax.axis_size("member"), lax.axis_index("member")
    partner = me + 1 - 2 * lax.rem(me, 2)

    def send(source, slot, order, to):
        return pltpu.make_async_remote_copy(
            src_ref=source,
            dst_ref=slots_ref.at[slot],
            send_sem=send_sem.at[order],
            recv_sem=recv_sem.at[order],
            device_id={"member": to},
            device_id_type=MESH,
        )

    half = axis // 2
    first = [
        send(own_ref, me, d - 1, lax.rem(me + 2 * d, axis)) for d in range(1, half)
    ]
    across = send(own_ref, me, half - 1, partner)
    passed = []
    for d in range(1, half):
        came = lax.rem(me - 2 * d + axis, axis)
        passed.append(send(slots_ref.at[came], came, half + d - 1, partner))
    return first, across, passed


def field_kernel(
    tile_cells, loc_ref, control_ref, pert_ref, points_ref, weights_ref, azimuth_ref,
    elevation_ref, innovation_ref, obs_ref, count_ref,
    field_ref, meta_ref, index_ref, counts_ref, side_ref,
    padded, pert_rows, loc_pad, own_ref, slots_ref, send_sem, recv_sem,
):
    axis, fields, slots = slots_ref.shape
    per = slots // LANES
    me = lax.axis_index("member")
    step = pl.program_id(0)

    @pl.when(step == 0)
    def _():
        padded[...] = jnp.zeros_like(padded)
        pad_matrix(loc_ref, loc_pad)
        own_ref[0:8, :] = weights_ref[...]
        horizontal = jnp.cos(elevation_ref[...])
        own_ref[8:9, :] = horizontal * jnp.sin(azimuth_ref[...])
        own_ref[9:10, :] = horizontal * jnp.cos(azimuth_ref[...])
        own_ref[10:11, :] = jnp.sin(elevation_ref[...])
        own_ref[11:12, :] = innovation_ref[...]
        own_ref[12:13, :] = obs_ref[...]
        own_ref[13:14, :] = points_ref[0:1, :].astype(jnp.float32)
        own_ref[14:15, :] = jnp.full((1, slots), count_ref[0], jnp.int32).astype(jnp.float32)
        own_ref[15:16, :] = jnp.zeros((1, slots), jnp.float32)
        greet()
        first, across_copy, passed = block_copies(own_ref, slots_ref, send_sem, recv_sem)
        for copy in first:
            copy.start()
        across_copy.start()
        slots_ref[me] = own_ref[...]

    levels, across, lanes = control_ref.shape
    control_rows = control_ref.reshape(levels * across, lanes)
    for r in range(across):
        padded[0:levels, r * LANES : (r + 1) * LANES] = control_rows[
            pl.ds(r, levels, stride=across), :
        ]
    localized = level_product(loc_pad[...], padded[...], False)[0:levels]
    members = across // X_BLOCK
    for c in range(3):
        pert_rows[...] = pert_ref[c].astype(jnp.float32).reshape(levels * across, lanes)
        for x in range(X_BLOCK):
            total = None
            for k in range(members):
                r = x * members + k
                term = (
                    pert_rows[pl.ds(r, levels, stride=across), :]
                    * localized[:, r * LANES : (r + 1) * LANES]
                )
                total = term if k == 0 else total + term
            if c == 0:
                field_ref[x * X_STEP + 144 : (x + 1) * X_STEP, :] = jnp.zeros(
                    (X_STEP - 144, LANES), jnp.float32
                )
            field_ref[pl.ds(x * X_STEP + c, levels, stride=3), :] = total

    @pl.when(step == FORWARD_STEP)
    def _():
        first, across_copy, passed = block_copies(own_ref, slots_ref, send_sem, recv_sem)
        for came, on in zip(first, passed):
            came.wait_recv()
            on.start()

    @pl.when(step == pl.num_programs(0) - 1)
    def _():
        first, across_copy, passed = block_copies(own_ref, slots_ref, send_sem, recv_sem)
        for copy in first:
            copy.wait_send()
        across_copy.wait()
        for copy in passed:
            copy.wait()
        slot = lax.broadcasted_iota(jnp.int32, (1, slots), 1)
        for d in range(axis):
            meta_ref[d] = slots_ref[d]
            base = slots_ref[d, 13:14, :].astype(jnp.int32)
            count = slots_ref[d, 14:15, :].astype(jnp.int32)
            level = lax.div(base, jnp.int32(tile_cells))
            inside = base - level * tile_cells
            column = lax.div(inside, jnp.int32(LANES))
            position = inside - column * LANES
            index = (column * LEVEL_PAD + level) * (3 * LANES) + ((slot - position) & (LANES - 1))
            live = jnp.where(slot < count, 1.0, 0.0)
            innovation = slots_ref[d, 11:12, :]
            weight = slots_ref[d, 12:13, :]
            counts_ref[d : d + 1, :] = count[:, 0:LANES]
            for q in range(per):
                row = d * per + q
                at = slice(q * LANES, (q + 1) * LANES)
                index_ref[row : row + 1, :] = index[:, at]
                side_ref[0, row : row + 1, :] = live[:, at]
                side_ref[1, row : row + 1, :] = innovation[:, at]
                side_ref[2, row : row + 1, :] = weight[:, at]


def residual_kernel(
    factor, partial_ref, side_ref, weighted_ref, residual_ref,
    parts_ref, done_ref, send_sem, recv_sem, send_done, recv_done,
):
    axis, per, lanes = parts_ref.shape
    me = lax.axis_index("member")
    greet()
    sums = copies_out(
        lambda to: partial_ref.at[pl.ds(pl.multiple_of(to * per, per), per), :],
        parts_ref, send_sem, recv_sem,
    )
    for copy in sums:
        copy.start()
    own = pl.ds(pl.multiple_of(me * per, per), per)
    parts_ref[me] = partial_ref[own, :]
    for copy in sums:
        copy.wait()
    total = parts_ref[0]
    for d in range(1, axis):
        total = total + parts_ref[d]
    residual = side_ref[0, own, :] * (factor * total - side_ref[1, own, :])
    residual_ref[...] = residual
    done_ref[me] = side_ref[2, own, :] * residual
    results = copies_out(lambda to: done_ref.at[me], done_ref, send_done, recv_done)
    for copy in results:
        copy.start()
    for copy in results:
        copy.wait()
    for d in range(axis):
        weighted_ref[d * per : (d + 1) * per, :] = done_ref[d]


def gate_factors(meta_ref, block, lanes):
    weight = meta_ref[block, 0:8, lanes]
    coeff = meta_ref[block, 8:16, lanes]
    row = lax.broadcasted_iota(jnp.int32, (8, LANES), 0)
    component = row % 3
    by_row = jnp.where(
        component == 0, coeff[0:1], jnp.where(component == 1, coeff[1:2], coeff[2:3])
    )
    factors = {}
    for b in range(2):
        for c in range(2):
            p = 2 * b + c
            corner = jnp.where(
                row < 3, weight[p : p + 1], jnp.where(row < 6, weight[4 + p : 5 + p], 0.0)
            )
            factors[b, c] = corner * by_row
    return factors


def over_groups(counts_ref, slots, visit):
    def block_body(block, carry):
        count = counts_ref[block * LANES]

        def group_body(group, inner):
            left = jnp.minimum(count - group * LANES, LANES)
            visit(block, group, (left + CHUNK - 1) // CHUNK)
            return inner

        lax.fori_loop(0, (count + LANES - 1) // LANES, group_body, 0)
        return carry

    lax.fori_loop(0, counts_ref.shape[0] // LANES, block_body, 0)


def gather_kernel(counts_ref, index_ref, meta_ref, field_ref, out_ref):
    slots = meta_ref.shape[2]
    groups = slots // LANES
    out_ref[...] = jnp.zeros_like(out_ref)
    lane = lax.broadcasted_iota(jnp.int32, (8, LANES), 1)

    def visit(block, group, chunks):
        first = block * slots + group * LANES

        def chunk_body(chunk, acc):
            a00, a01, a10, a11 = acc
            slot = chunk * CHUNK
            shifted = lane - slot
            here = shifted == 0
            for i in range(CHUNK):
                packed = index_ref[first + slot + i]
                row = packed >> 7
                shift = packed & 127
                near = pltpu.roll(field_ref[pl.ds(row, 8), :], shift, axis=1)
                far = pltpu.roll(field_ref[pl.ds(row + X_STEP, 8), :], shift, axis=1)
                if i < CHUNK - 1:
                    after = shifted == i + 1
                else:
                    after = lane == ((slot + CHUNK) & 127)
                a00 = jnp.where(here, near, a00)
                a01 = jnp.where(after, near, a01)
                a10 = jnp.where(here, far, a10)
                a11 = jnp.where(after, far, a11)
                here = after
            return a00, a01, a10, a11

        zero = jnp.zeros((8, LANES), jnp.float32)
        a00, a01, a10, a11 = lax.fori_loop(0, chunks, chunk_body, (zero, zero, zero, zero))
        factors = gate_factors(meta_ref, block, pl.ds(pl.multiple_of(group * LANES, LANES), LANES))
        value = (
            a00 * factors[0, 0]
            + pltpu.roll(a01, LANES - 1, axis=1) * factors[0, 1]
            + a10 * factors[1, 0]
            + pltpu.roll(a11, LANES - 1, axis=1) * factors[1, 1]
        )
        out_ref[pl.ds(block * groups + group, 1), :] = jnp.sum(value, axis=0, keepdims=True)

    over_groups(counts_ref, slots, visit)


def scatter_kernel(
    factor, counts_ref, index_ref, meta_ref, weighted_ref, loc_ref, control_ref, pert_ref,
    out_ref, buffers, padded, pert_rows, loc_pad,
):
    levels, across, lanes = control_ref.shape
    slots = meta_ref.shape[2]
    groups = slots // LANES
    step = pl.program_id(0)

    @pl.when(step == 0)
    def _():
        padded[...] = jnp.zeros_like(padded)
        pad_matrix(loc_ref, loc_pad)
        rows = buffers.shape[1]
        per = X_STEP

        def clear(i, carry):
            at = pl.ds(pl.multiple_of(i * per, per), per)
            for j in range(BUFFERS):
                buffers[j, at, :] = jnp.zeros((per, LANES), jnp.float32)
            return carry

        lax.fori_loop(0, rows // per, clear, 0)
        lane = lax.broadcasted_iota(jnp.int32, (8, LANES), 1)

        def visit(block, group, chunks):
            first = block * slots + group * LANES
            factors = gate_factors(
                meta_ref, block, pl.ds(pl.multiple_of(group * LANES, LANES), LANES)
            )
            amount = weighted_ref[pl.ds(block * groups + group, 1), :]
            a00 = factors[0, 0] * amount
            a01 = pltpu.roll(factors[0, 1] * amount, 1, axis=1)
            a10 = factors[1, 0] * amount
            a11 = pltpu.roll(factors[1, 1] * amount, 1, axis=1)

            def chunk_body(chunk, carry):
                slot = chunk * CHUNK
                shifted = lane - slot
                here = shifted == 0
                for i0 in range(0, CHUNK, BUFFERS):
                    added = []
                    for j in range(BUFFERS):
                        i = i0 + j
                        packed = index_ref[first + slot + i]
                        row = packed >> 7
                        shift = (-packed) & 127
                        if i < CHUNK - 1:
                            after = shifted == i + 1
                        else:
                            after = lane == ((slot + CHUNK) & 127)
                        near = jnp.where(here, a00, jnp.where(after, a01, 0.0))
                        far = jnp.where(here, a10, jnp.where(after, a11, 0.0))
                        here = after
                        added.append(
                            (
                                pl.ds(row, 8),
                                pl.ds(row + X_STEP, 8),
                                pltpu.roll(near, shift, axis=1),
                                pltpu.roll(far, shift, axis=1),
                            )
                        )
                    held = [
                        (buffers[j, added[j][0], :], buffers[j, added[j][1], :])
                        for j in range(BUFFERS)
                    ]
                    for j in range(BUFFERS):
                        buffers[j, added[j][0], :] = held[j][0] + added[j][2]
                        buffers[j, added[j][1], :] = held[j][1] + added[j][3]
                return carry

            lax.fori_loop(0, chunks, chunk_body, 0)

        over_groups(counts_ref, slots, visit)

    members = across // X_BLOCK
    for c in range(3):
        pert_rows[...] = pert_ref[c].astype(jnp.float32).reshape(levels * across, lanes)
        for x in range(X_BLOCK):
            at = pl.ds((step * X_BLOCK + x) * X_STEP + c, levels, stride=3)
            adjoint = buffers[0, at, :]
            for j in range(1, BUFFERS):
                adjoint = adjoint + buffers[j, at, :]
            for k in range(members):
                r = x * members + k
                here = slice(r * LANES, (r + 1) * LANES)
                term = pert_rows[pl.ds(r, levels, stride=across), :] * adjoint
                if c == 0:
                    padded[0:levels, here] = term
                else:
                    padded[0:levels, here] = padded[0:levels, here] + term
    product = level_product(loc_pad[...], padded[...], True)
    control_rows = control_ref.reshape(levels * across, lanes)
    out_rows = out_ref.reshape(levels * across, lanes)
    for r in range(across):
        at = pl.ds(r, levels, stride=across)
        out_rows[at, :] = (
            control_rows[at, :] + factor * product[0:levels, r * LANES : (r + 1) * LANES]
        )


def whole(shape):
    return pl.BlockSpec(shape, lambda *i: (0,) * len(shape))


def local(
    perturbations,
    control,
    loc_sqrt,
    gate_points,
    gate_weights,
    gate_azimuth,
    gate_elevation,
    innovation,
    obs_weight,
    gate_counts,
):
    mem_dev, components, levels, tile_cells = perturbations.shape
    slots = gate_points.shape[1]
    axis = lax.axis_size("member")
    factor = (mem_dev * axis - 1) ** (-0.5)
    columns = tile_cells // LANES
    rows = columns * X_STEP
    groups = axis * slots // LANES
    vmem = pl.BlockSpec(memory_space=pltpu.VMEM)
    smem = pl.BlockSpec(memory_space=pltpu.SMEM)
    semaphores = [pltpu.SemaphoreType.DMA((axis - 1,)), pltpu.SemaphoreType.DMA((axis - 1,))]
    across = X_BLOCK * mem_dev
    control_view = (
        control.reshape(mem_dev, levels, columns, LANES)
        .transpose(1, 2, 0, 3)
        .reshape(levels, columns * mem_dev, LANES)
    )
    pert_view = (
        perturbations.reshape(mem_dev, 3, levels, columns, LANES)
        .transpose(1, 2, 3, 0, 4)
        .reshape(3, levels, columns * mem_dev, LANES)
    )
    pert_spec = pl.BlockSpec((3, levels, across, LANES), lambda i: (0, 0, i, 0))
    control_spec = pl.BlockSpec((levels, across, LANES), lambda i: (0, i, 0))
    dense = [
        pltpu.VMEM((DEPTH, across * LANES), jnp.float32),
        pltpu.VMEM((levels * across, LANES), jnp.float32),
        pltpu.VMEM((DEPTH, DEPTH), jnp.float32),
    ]
    row = whole((1, slots))
    field, meta, index, counts, side = pl.pallas_call(
        functools.partial(field_kernel, tile_cells),
        grid=(columns // X_BLOCK,),
        out_shape=(
            jax.ShapeDtypeStruct((rows, LANES), jnp.float32),
            jax.ShapeDtypeStruct((axis, 16, slots), jnp.float32),
            jax.ShapeDtypeStruct((groups, LANES), jnp.int32),
            jax.ShapeDtypeStruct((axis, LANES), jnp.int32),
            jax.ShapeDtypeStruct((3, groups, LANES), jnp.float32),
        ),
        in_specs=[
            whole((levels, levels)),
            control_spec,
            pert_spec,
            whole((8, slots)),
            whole((8, slots)),
            row,
            row,
            row,
            row,
            smem,
        ],
        out_specs=(
            pl.BlockSpec((X_BLOCK * X_STEP, LANES), lambda i: (i, 0)),
            whole((axis, 16, slots)),
            whole((groups, LANES)),
            whole((axis, LANES)),
            whole((3, groups, LANES)),
        ),
        scratch_shapes=[
            *dense,
            pltpu.VMEM((16, slots), jnp.float32),
            pltpu.VMEM((axis, 16, slots), jnp.float32),
            *semaphores,
        ],
        compiler_params=pltpu.CompilerParams(
            collective_id=0, has_side_effects=True, vmem_limit_bytes=VMEM
        ),
        name="field",
    )(
        loc_sqrt,
        control_view,
        pert_view,
        gate_points,
        gate_weights,
        gate_azimuth.reshape(1, slots),
        gate_elevation.reshape(1, slots),
        innovation.reshape(1, slots),
        obs_weight.reshape(1, slots),
        gate_counts,
    )
    index, counts = index.reshape(-1), counts.reshape(-1)

    partial = pl.pallas_call(
        gather_kernel,
        out_shape=jax.ShapeDtypeStruct((groups, LANES), jnp.float32),
        in_specs=[smem, smem, vmem, vmem],
        out_specs=vmem,
        compiler_params=pltpu.CompilerParams(vmem_limit_bytes=VMEM),
        name="gather",
    )(counts, index, meta, field)

    weighted, residual = pl.pallas_call(
        functools.partial(residual_kernel, factor),
        out_shape=(
            jax.ShapeDtypeStruct((groups, LANES), jnp.float32),
            jax.ShapeDtypeStruct((slots // LANES, LANES), jnp.float32),
        ),
        in_specs=[vmem, vmem],
        out_specs=(vmem, vmem),
        scratch_shapes=[
            pltpu.VMEM((axis, slots // LANES, LANES), jnp.float32),
            pltpu.VMEM((axis, slots // LANES, LANES), jnp.float32),
            *semaphores,
            *semaphores,
        ],
        compiler_params=pltpu.CompilerParams(
            collective_id=1, has_side_effects=True, vmem_limit_bytes=VMEM
        ),
        name="residual",
    )(partial, side)
    gate_residual = residual.reshape(slots)

    gradient = pl.pallas_call(
        functools.partial(scatter_kernel, factor),
        grid=(columns // X_BLOCK,),
        out_shape=jax.ShapeDtypeStruct((levels, columns * mem_dev, LANES), jnp.float32),
        in_specs=[
            smem,
            smem,
            whole(meta.shape),
            whole((groups, LANES)),
            whole((levels, levels)),
            control_spec,
            pert_spec,
        ],
        out_specs=control_spec,
        scratch_shapes=[
            pltpu.VMEM((BUFFERS, rows, LANES), jnp.float32),
            *dense,
        ],
        compiler_params=pltpu.CompilerParams(vmem_limit_bytes=VMEM),
        name="scatter",
    )(counts, index, meta, weighted, loc_sqrt, control_view, pert_view)
    gradient = (
        gradient.reshape(levels, columns, mem_dev, LANES)
        .transpose(2, 0, 1, 3)
        .reshape(mem_dev, levels, tile_cells)
    )
    return (gradient, gate_residual)


def solution(mesh):
    by_gate = P(("groups", "member", "tile"))
    return jax.shard_map(
        local,
        mesh=mesh,
        in_specs=(
            P(("groups", "member"), None, None, "tile"),
            P(("groups", "member"), None, "tile"),
            P(),
            P(None, ("groups", "member", "tile")),
            P(None, ("groups", "member", "tile")),
            by_gate,
            by_gate,
            by_gate,
            by_gate,
            by_gate,
        ),
        out_specs=(P(("groups", "member"), None, "tile"), by_gate),
        check_vma=False,
    )
```

```python
import functools

import jax
import jax.numpy as jnp
from jax import lax
from jax.experimental import pallas as pl
from jax.experimental.pallas import tpu as pltpu
from jax.sharding import PartitionSpec as P

LANES = 128
LEVEL_PAD = 56
DEPTH = 64
X_STEP = LEVEL_PAD * 3
CHUNK = 128
BUFFERS = 4
X_BLOCK = 16
FORWARD_STEP = 2
MESH = pl.DeviceIdType.MESH
VMEM = 56 * 1024 * 1024


def split(value):
    high = value.astype(jnp.bfloat16)
    low = (value - high.astype(jnp.float32)).astype(jnp.bfloat16)
    return high, low


def level_product(matrix, value, flipped):
    m_high, m_low = split(matrix)
    v_high, v_low = split(value)
    side = 0 if flipped else 1
    left = jnp.concatenate([m_high, m_high, m_low], axis=side)
    right = jnp.concatenate([v_high, v_low, v_high], axis=0)
    return lax.dot_general(
        left, right, (((side,), (0,)), ((), ())), preferred_element_type=jnp.float32
    )


def pad_matrix(loc_ref, loc_pad):
    levels = loc_ref.shape[0]
    loc_pad[...] = jnp.zeros_like(loc_pad)
    loc_pad[0:levels, 0:levels] = loc_ref[...]


def greet():
    axis, me = lax.axis_size("member"), lax.axis_index("member")
    barrier = pltpu.get_barrier_semaphore()
    for d in range(1, axis):
        pl.semaphore_signal(
            barrier, inc=1, device_id={"member": lax.rem(me + d, axis)}, device_id_type=MESH
        )
    pl.semaphore_wait(barrier, axis - 1)


def copies_out(source, slots_ref, send_sem, recv_sem):
    axis, me = lax.axis_size("member"), lax.axis_index("member")
    copies = []
    for d in range(1, axis):
        to = lax.rem(me + d, axis)
        copies.append(
            pltpu.make_async_remote_copy(
                src_ref=source(to),
                dst_ref=slots_ref.at[me],
                send_sem=send_sem.at[d - 1],
                recv_sem=recv_sem.at[d - 1],
                device_id={"member": to},
                device_id_type=MESH,
            )
        )
    return copies


def block_copies(own_ref, slots_ref, send_sem, recv_sem):
    axis, me = lax.axis_size("member"), lax.axis_index("member")
    partner = me + 1 - 2 * lax.rem(me, 2)

    def send(source, slot, order, to):
        return pltpu.make_async_remote_copy(
            src_ref=source,
            dst_ref=slots_ref.at[slot],
            send_sem=send_sem.at[order],
            recv_sem=recv_sem.at[order],
            device_id={"member": to},
            device_id_type=MESH,
        )

    half = axis // 2
    first = [
        send(own_ref, me, d - 1, lax.rem(me + 2 * d, axis)) for d in range(1, half)
    ]
    across = send(own_ref, me, half - 1, partner)
    passed = []
    for d in range(1, half):
        came = lax.rem(me - 2 * d + axis, axis)
        passed.append(send(slots_ref.at[came], came, half + d - 1, partner))
    return first, across, passed


def field_kernel(
    tile_cells, loc_ref, control_ref, pert_ref, points_ref, weights_ref, azimuth_ref,
    elevation_ref, innovation_ref, obs_ref, count_ref,
    field_ref, meta_ref, index_ref, counts_ref, side_ref,
    padded, pert_rows, loc_pad, own_ref, slots_ref, send_sem, recv_sem,
):
    axis, fields, slots = slots_ref.shape
    per = slots // LANES
    me = lax.axis_index("member")
    step = pl.program_id(0)

    @pl.when(step == 0)
    def _():
        padded[...] = jnp.zeros_like(padded)
        pad_matrix(loc_ref, loc_pad)
        own_ref[0:8, :] = weights_ref[...]
        horizontal = jnp.cos(elevation_ref[...])
        own_ref[8:9, :] = horizontal * jnp.sin(azimuth_ref[...])
        own_ref[9:10, :] = horizontal * jnp.cos(azimuth_ref[...])
        own_ref[10:11, :] = jnp.sin(elevation_ref[...])
        own_ref[11:12, :] = innovation_ref[...]
        own_ref[12:13, :] = obs_ref[...]
        own_ref[13:14, :] = points_ref[0:1, :].astype(jnp.float32)
        own_ref[14:15, :] = jnp.full((1, slots), count_ref[0], jnp.int32).astype(jnp.float32)
        own_ref[15:16, :] = jnp.zeros((1, slots), jnp.float32)
        greet()
        first, across_copy, passed = block_copies(own_ref, slots_ref, send_sem, recv_sem)
        for copy in first:
            copy.start()
        across_copy.start()
        slots_ref[me] = own_ref[...]

    levels, across, lanes = control_ref.shape
    control_rows = control_ref.reshape(levels * across, lanes)
    for r in range(across):
        padded[0:levels, r * LANES : (r + 1) * LANES] = control_rows[
            pl.ds(r, levels, stride=across), :
        ]
    localized = level_product(loc_pad[...], padded[...], False)[0:levels]
    members = across // X_BLOCK
    for c in range(3):
        pert_rows[...] = pert_ref[c].astype(jnp.float32).reshape(levels * across, lanes)
        for x in range(X_BLOCK):
            total = None
            for k in range(members):
                r = x * members + k
                term = (
                    pert_rows[pl.ds(r, levels, stride=across), :]
                    * localized[:, r * LANES : (r + 1) * LANES]
                )
                total = term if k == 0 else total + term
            if c == 0:
                field_ref[x * X_STEP + 144 : (x + 1) * X_STEP, :] = jnp.zeros(
                    (X_STEP - 144, LANES), jnp.float32
                )
            field_ref[pl.ds(x * X_STEP + c, levels, stride=3), :] = total

    @pl.when(step == FORWARD_STEP)
    def _():
        first, across_copy, passed = block_copies(own_ref, slots_ref, send_sem, recv_sem)
        for came, on in zip(first, passed):
            came.wait_recv()
            on.start()

    @pl.when(step == pl.num_programs(0) - 1)
    def _():
        first, across_copy, passed = block_copies(own_ref, slots_ref, send_sem, recv_sem)
        for copy in first:
            copy.wait_send()
        across_copy.wait()
        for copy in passed:
            copy.wait()
        slot = lax.broadcasted_iota(jnp.int32, (1, slots), 1)
        for d in range(axis):
            meta_ref[d] = slots_ref[d]
            base = slots_ref[d, 13:14, :].astype(jnp.int32)
            count = slots_ref[d, 14:15, :].astype(jnp.int32)
            level = lax.div(base, jnp.int32(tile_cells))
            inside = base - level * tile_cells
            column = lax.div(inside, jnp.int32(LANES))
            position = inside - column * LANES
            index = (column * LEVEL_PAD + level) * (3 * LANES) + ((slot - position) & (LANES - 1))
            live = jnp.where(slot < count, 1.0, 0.0)
            innovation = slots_ref[d, 11:12, :]
            weight = slots_ref[d, 12:13, :]
            counts_ref[d : d + 1, :] = count[:, 0:LANES]
            for q in range(per):
                row = d * per + q
                at = slice(q * LANES, (q + 1) * LANES)
                index_ref[row : row + 1, :] = index[:, at]
                side_ref[0, row : row + 1, :] = live[:, at]
                side_ref[1, row : row + 1, :] = innovation[:, at]
                side_ref[2, row : row + 1, :] = weight[:, at]


def residual_kernel(
    factor, partial_ref, side_ref, weighted_ref, residual_ref,
    parts_ref, done_ref, send_sem, recv_sem, send_done, recv_done,
):
    axis, per, lanes = parts_ref.shape
    me = lax.axis_index("member")
    greet()
    sums = copies_out(
        lambda to: partial_ref.at[pl.ds(pl.multiple_of(to * per, per), per), :],
        parts_ref, send_sem, recv_sem,
    )
    for copy in sums:
        copy.start()
    own = pl.ds(pl.multiple_of(me * per, per), per)
    parts_ref[me] = partial_ref[own, :]
    for copy in sums:
        copy.wait()
    total = parts_ref[0]
    for d in range(1, axis):
        total = total + parts_ref[d]
    residual = side_ref[0, own, :] * (factor * total - side_ref[1, own, :])
    residual_ref[...] = residual
    done_ref[me] = side_ref[2, own, :] * residual
    results = copies_out(lambda to: done_ref.at[me], done_ref, send_done, recv_done)
    for copy in results:
        copy.start()
    for copy in results:
        copy.wait()
    for d in range(axis):
        weighted_ref[d * per : (d + 1) * per, :] = done_ref[d]


def gate_factors(meta_ref, block, lanes):
    weight = meta_ref[block, 0:8, lanes]
    coeff = meta_ref[block, 8:16, lanes]
    row = lax.broadcasted_iota(jnp.int32, (8, LANES), 0)
    component = row % 3
    by_row = jnp.where(
        component == 0, coeff[0:1], jnp.where(component == 1, coeff[1:2], coeff[2:3])
    )
    factors = {}
    for b in range(2):
        for c in range(2):
            p = 2 * b + c
            corner = jnp.where(
                row < 3, weight[p : p + 1], jnp.where(row < 6, weight[4 + p : 5 + p], 0.0)
            )
            factors[b, c] = corner * by_row
    return factors


def over_groups(counts_ref, slots, visit):
    def block_body(block, carry):
        count = counts_ref[block * LANES]

        def group_body(group, inner):
            left = jnp.minimum(count - group * LANES, LANES)
            visit(block, group, (left + CHUNK - 1) // CHUNK)
            return inner

        lax.fori_loop(0, (count + LANES - 1) // LANES, group_body, 0)
        return carry

    lax.fori_loop(0, counts_ref.shape[0] // LANES, block_body, 0)


def gather_kernel(counts_ref, index_ref, meta_ref, field_ref, out_ref):
    slots = meta_ref.shape[2]
    groups = slots // LANES
    out_ref[...] = jnp.zeros_like(out_ref)
    lane = lax.broadcasted_iota(jnp.int32, (8, LANES), 1)

    def visit(block, group, chunks):
        first = block * slots + group * LANES

        def chunk_body(chunk, acc):
            a00, a01, a10, a11 = acc
            slot = chunk * CHUNK
            shifted = lane - slot
            here = shifted == 0
            for i in range(CHUNK):
                packed = index_ref[first + slot + i]
                row = packed >> 7
                shift = packed & 127
                near = pltpu.roll(field_ref[pl.ds(row, 8), :], shift, axis=1)
                far = pltpu.roll(field_ref[pl.ds(row + X_STEP, 8), :], shift, axis=1)
                if i < CHUNK - 1:
                    after = shifted == i + 1
                else:
                    after = lane == ((slot + CHUNK) & 127)
                a00 = jnp.where(here, near, a00)
                a01 = jnp.where(after, near, a01)
                a10 = jnp.where(here, far, a10)
                a11 = jnp.where(after, far, a11)
                here = after
            return a00, a01, a10, a11

        zero = jnp.zeros((8, LANES), jnp.float32)
        a00, a01, a10, a11 = lax.fori_loop(0, chunks, chunk_body, (zero, zero, zero, zero))
        factors = gate_factors(meta_ref, block, pl.ds(pl.multiple_of(group * LANES, LANES), LANES))
        value = (
            a00 * factors[0, 0]
            + pltpu.roll(a01, LANES - 1, axis=1) * factors[0, 1]
            + a10 * factors[1, 0]
            + pltpu.roll(a11, LANES - 1, axis=1) * factors[1, 1]
        )
        out_ref[pl.ds(block * groups + group, 1), :] = jnp.sum(value, axis=0, keepdims=True)

    over_groups(counts_ref, slots, visit)


def scatter_kernel(
    factor, counts_ref, index_ref, meta_ref, weighted_ref, loc_ref, control_ref, pert_ref,
    out_ref, buffers, padded, pert_rows, loc_pad,
):
    levels, across, lanes = control_ref.shape
    slots = meta_ref.shape[2]
    groups = slots // LANES
    step = pl.program_id(0)

    @pl.when(step == 0)
    def _():
        padded[...] = jnp.zeros_like(padded)
        pad_matrix(loc_ref, loc_pad)
        rows = buffers.shape[1]
        per = X_STEP

        def clear(i, carry):
            at = pl.ds(pl.multiple_of(i * per, per), per)
            for j in range(BUFFERS):
                buffers[j, at, :] = jnp.zeros((per, LANES), jnp.float32)
            return carry

        lax.fori_loop(0, rows // per, clear, 0)
        lane = lax.broadcasted_iota(jnp.int32, (8, LANES), 1)

        def visit(block, group, chunks):
            first = block * slots + group * LANES
            factors = gate_factors(
                meta_ref, block, pl.ds(pl.multiple_of(group * LANES, LANES), LANES)
            )
            amount = weighted_ref[pl.ds(block * groups + group, 1), :]
            a00 = factors[0, 0] * amount
            a01 = pltpu.roll(factors[0, 1] * amount, 1, axis=1)
            a10 = factors[1, 0] * amount
            a11 = pltpu.roll(factors[1, 1] * amount, 1, axis=1)

            def chunk_body(chunk, carry):
                slot = chunk * CHUNK
                shifted = lane - slot
                here = shifted == 0
                for i0 in range(0, CHUNK, BUFFERS):
                    added = []
                    for j in range(BUFFERS):
                        i = i0 + j
                        packed = index_ref[first + slot + i]
                        row = packed >> 7
                        shift = (-packed) & 127
                        if i < CHUNK - 1:
                            after = shifted == i + 1
                        else:
                            after = lane == ((slot + CHUNK) & 127)
                        near = jnp.where(here, a00, jnp.where(after, a01, 0.0))
                        far = jnp.where(here, a10, jnp.where(after, a11, 0.0))
                        here = after
                        added.append(
                            (
                                pl.ds(row, 8),
                                pl.ds(row + X_STEP, 8),
                                pltpu.roll(near, shift, axis=1),
                                pltpu.roll(far, shift, axis=1),
                            )
                        )
                    held = [
                        (buffers[j, added[j][0], :], buffers[j, added[j][1], :])
                        for j in range(BUFFERS)
                    ]
                    for j in range(BUFFERS):
                        buffers[j, added[j][0], :] = held[j][0] + added[j][2]
                        buffers[j, added[j][1], :] = held[j][1] + added[j][3]
                return carry

            lax.fori_loop(0, chunks, chunk_body, 0)

        over_groups(counts_ref, slots, visit)

    members = across // X_BLOCK
    for c in range(3):
        pert_rows[...] = pert_ref[c].astype(jnp.float32).reshape(levels * across, lanes)
        for x in range(X_BLOCK):
            at = pl.ds((step * X_BLOCK + x) * X_STEP + c, levels, stride=3)
            adjoint = buffers[0, at, :]
            for j in range(1, BUFFERS):
                adjoint = adjoint + buffers[j, at, :]
            for k in range(members):
                r = x * members + k
                here = slice(r * LANES, (r + 1) * LANES)
                term = pert_rows[pl.ds(r, levels, stride=across), :] * adjoint
                if c == 0:
                    padded[0:levels, here] = term
                else:
                    padded[0:levels, here] = padded[0:levels, here] + term
    product = level_product(loc_pad[...], padded[...], True)
    control_rows = control_ref.reshape(levels * across, lanes)
    out_rows = out_ref.reshape(levels * across, lanes)
    for r in range(across):
        at = pl.ds(r, levels, stride=across)
        out_rows[at, :] = (
            control_rows[at, :] + factor * product[0:levels, r * LANES : (r + 1) * LANES]
        )


def whole(shape):
    return pl.BlockSpec(shape, lambda *i: (0,) * len(shape))


def local(
    perturbations,
    control,
    loc_sqrt,
    gate_points,
    gate_weights,
    gate_azimuth,
    gate_elevation,
    innovation,
    obs_weight,
    gate_counts,
):
    mem_dev, components, levels, tile_cells = perturbations.shape
    slots = gate_points.shape[1]
    axis = lax.axis_size("member")
    factor = (mem_dev * axis - 1) ** (-0.5)
    columns = tile_cells // LANES
    rows = columns * X_STEP
    groups = axis * slots // LANES
    vmem = pl.BlockSpec(memory_space=pltpu.VMEM)
    smem = pl.BlockSpec(memory_space=pltpu.SMEM)
    semaphores = [pltpu.SemaphoreType.DMA((axis - 1,)), pltpu.SemaphoreType.DMA((axis - 1,))]
    across = X_BLOCK * mem_dev
    control_view = (
        control.reshape(mem_dev, levels, columns, LANES)
        .transpose(1, 2, 0, 3)
        .reshape(levels, columns * mem_dev, LANES)
    )
    pert_view = (
        perturbations.reshape(mem_dev, 3, levels, columns, LANES)
        .transpose(1, 2, 3, 0, 4)
        .reshape(3, levels, columns * mem_dev, LANES)
    )
    pert_spec = pl.BlockSpec((3, levels, across, LANES), lambda i: (0, 0, i, 0))
    control_spec = pl.BlockSpec((levels, across, LANES), lambda i: (0, i, 0))
    dense = [
        pltpu.VMEM((DEPTH, across * LANES), jnp.float32),
        pltpu.VMEM((levels * across, LANES), jnp.float32),
        pltpu.VMEM((DEPTH, DEPTH), jnp.float32),
    ]
    row = whole((1, slots))
    field, meta, index, counts, side = pl.pallas_call(
        functools.partial(field_kernel, tile_cells),
        grid=(columns // X_BLOCK,),
        out_shape=(
            jax.ShapeDtypeStruct((rows, LANES), jnp.float32),
            jax.ShapeDtypeStruct((axis, 16, slots), jnp.float32),
            jax.ShapeDtypeStruct((groups, LANES), jnp.int32),
            jax.ShapeDtypeStruct((axis, LANES), jnp.int32),
            jax.ShapeDtypeStruct((3, groups, LANES), jnp.float32),
        ),
        in_specs=[
            whole((levels, levels)),
            control_spec,
            pert_spec,
            whole((8, slots)),
            whole((8, slots)),
            row,
            row,
            row,
            row,
            smem,
        ],
        out_specs=(
            pl.BlockSpec((X_BLOCK * X_STEP, LANES), lambda i: (i, 0)),
            whole((axis, 16, slots)),
            whole((groups, LANES)),
            whole((axis, LANES)),
            whole((3, groups, LANES)),
        ),
        scratch_shapes=[
            *dense,
            pltpu.VMEM((16, slots), jnp.float32),
            pltpu.VMEM((axis, 16, slots), jnp.float32),
            *semaphores,
        ],
        compiler_params=pltpu.CompilerParams(
            collective_id=0, has_side_effects=True, vmem_limit_bytes=VMEM
        ),
        name="field",
    )(
        loc_sqrt,
        control_view,
        pert_view,
        gate_points,
        gate_weights,
        gate_azimuth.reshape(1, slots),
        gate_elevation.reshape(1, slots),
        innovation.reshape(1, slots),
        obs_weight.reshape(1, slots),
        gate_counts,
    )
    index, counts = index.reshape(-1), counts.reshape(-1)

    partial = pl.pallas_call(
        gather_kernel,
        out_shape=jax.ShapeDtypeStruct((groups, LANES), jnp.float32),
        in_specs=[smem, smem, vmem, vmem],
        out_specs=vmem,
        compiler_params=pltpu.CompilerParams(vmem_limit_bytes=VMEM),
        name="gather",
    )(counts, index, meta, field)

    weighted, residual = pl.pallas_call(
        functools.partial(residual_kernel, factor),
        out_shape=(
            jax.ShapeDtypeStruct((groups, LANES), jnp.float32),
            jax.ShapeDtypeStruct((slots // LANES, LANES), jnp.float32),
        ),
        in_specs=[vmem, vmem],
        out_specs=(vmem, vmem),
        scratch_shapes=[
            pltpu.VMEM((axis, slots // LANES, LANES), jnp.float32),
            pltpu.VMEM((axis, slots // LANES, LANES), jnp.float32),
            *semaphores,
            *semaphores,
        ],
        compiler_params=pltpu.CompilerParams(
            collective_id=1, has_side_effects=True, vmem_limit_bytes=VMEM
        ),
        name="residual",
    )(partial, side)
    gate_residual = residual.reshape(slots)

    gradient = pl.pallas_call(
        functools.partial(scatter_kernel, factor),
        grid=(columns // X_BLOCK,),
        out_shape=jax.ShapeDtypeStruct((levels, columns * mem_dev, LANES), jnp.float32),
        in_specs=[
            smem,
            smem,
            whole(meta.shape),
            whole((groups, LANES)),
            whole((levels, levels)),
            control_spec,
            pert_spec,
        ],
        out_specs=control_spec,
        scratch_shapes=[
            pltpu.VMEM((BUFFERS, rows, LANES), jnp.float32),
            *dense,
        ],
        compiler_params=pltpu.CompilerParams(vmem_limit_bytes=VMEM),
        name="scatter",
    )(counts, index, meta, weighted, loc_sqrt, control_view, pert_view)
    gradient = (
        gradient.reshape(levels, columns, mem_dev, LANES)
        .transpose(2, 0, 1, 3)
        .reshape(mem_dev, levels, tile_cells)
    )
    return (gradient, gate_residual)


def solution(mesh):
    by_gate = P(("groups", "member", "tile"))
    return jax.shard_map(
        local,
        mesh=mesh,
        in_specs=(
            P(("groups", "member"), None, None, "tile"),
            P(("groups", "member"), None, "tile"),
            P(),
            P(None, ("groups", "member", "tile")),
            P(None, ("groups", "member", "tile")),
            by_gate,
            by_gate,
            by_gate,
            by_gate,
            by_gate,
        ),
        out_specs=(P(("groups", "member"), None, "tile"), by_gate),
        check_vma=False,
    )
```
